32 devices in a mesh: dp: 8 (over z, x), dap: 4 (over y, core).
Axes of the slice: x: 2, y: 2, z: 4, core: 2. Of those that a mesh axis runs over, the one named last changes fastest.
Arguments:
- pair: bfloat16 [8, 64, 64, 128], P('dp', 'dap'), may hold values from -6 to 6
- pair_grad: bfloat16 [8, 64, 64, 128], P('dp', 'dap'), may hold values from -6 to 6
- token_mask: int32 [8, 64], P('dp'), may hold values from 0 to 1, as said below
- w_edges: bfloat16 [128, 512], replicated, may hold values from -0.5 to 0.5
- w_gate: bfloat16 [128, 128], replicated, may hold values from -0.5 to 0.5
- w_out: bfloat16 [128, 128], replicated, may hold values from -0.5 to 0.5
- in_gain: float32 [128], replicated, may hold values from 0.5 to 1.5
- in_bias: float32 [128], replicated, may hold values from -1.5 to 1.5
- output_norm_gain: float32 [128], replicated, may hold values from 0.5 to 1.5
- output_norm_bias: float32 [128], replicated, may hold values from -1.5 to 1.5
Outputs:
- pair_input_grad: bfloat16 [8, 64, 64, 128], P('dp', 'dap')
- grad_edges: float32 [128, 512], replicated
- grad_gate: float32 [128, 128], replicated
- grad_out: float32 [128, 128], replicated
- grad_in_norm: float32 [2, 128], replicated
- output_norm_param_grads: float32 [2, 128], replicated
The draws below stay inside these ranges and needn't reach their ends.
Inputs may be any that keep to these rules, and one draw needn't show every extreme that they name: `token_mask`: each structure's valid tokens are its first L tokens with L between 32 and 64; structure 0 has all 64 valid.
All inputs are finite; a program needn't handle non-finite values.
Results may differ from the reference program's by a relative error of at most 0.0093.
Values may be sent and summed in bfloat16 or wider, within the bound.
No kernel may reach another device: no remote copies, remote signals or barrier semaphores. Data moves between devices by JAX's collectives and lax.ppermute only.
A program may use at most 64 MiB of HBM per device.

```python
import jax
import jax.numpy as jnp
from jax import lax

C = 128
H = 128
N = 64
STRUCTS = 8


def draw_token_mask(key, part):
    lengths = jax.random.randint(key, (STRUCTS,), N // 2, N + 1)
    lengths = lengths.at[0].set(N)
    position = jnp.arange(N, dtype=jnp.int32)
    return (position[None, :] < lengths[:, None]).astype(jnp.int32)


def steps_of(stream_key, dims, pieces, low, high):
    def one(dim, shards_of):
        steps = jax.random.uniform(jax.random.fold_in(jax.random.fold_in(stream_key, 6), dim), (shards_of,), jnp.float32, low / len(pieces), high / len(pieces))
        return jnp.repeat(jnp.exp(steps), dims[dim] // shards_of).reshape((-1,) + (1,) * (len(dims) - dim - 1))

    factor_of = one(*pieces[0])
    for cut in pieces[1:]:
        factor_of = factor_of * one(*cut)
    return factor_of


def centred(own_key, dims, width, reach, cuts=(), held_as=jnp.bfloat16):
    entries = width * jax.random.normal(own_key, dims, jnp.float32)
    if cuts:
        entries = entries * steps_of(own_key, dims, cuts, -0.22, 0.18)
    return jnp.clip(entries, -reach, reach).astype(held_as)


def setup_inputs(seed: int = 0) -> dict:
    key_of = jax.random.split(jax.random.key(seed), 11)
    pair = centred(key_of[0], (STRUCTS, N, N, C), 1.0, 6.0, ((0, 8), (1, 4)))
    pair_grad = centred(key_of[1], (STRUCTS, N, N, C), 1.0, 6.0, ((0, 8), (1, 4)))
    token_mask = draw_token_mask(jax.random.fold_in(key_of[10], 71), 0)
    w_edges = centred(key_of[3], (C, 4 * H), C ** -0.5, 0.5)
    w_gate = centred(key_of[4], (C, C), C ** -0.5, 0.5)
    w_out = centred(key_of[5], (H, C), H ** -0.5, 0.5)
    in_gain = jnp.clip(1.0 + 0.1 * jax.random.normal(key_of[6], (C,), jnp.float32), 0.5, 1.5)
    in_bias = centred(key_of[7], (C,), 0.3, 1.5, (), jnp.float32)
    output_norm_gain = jnp.clip(1.0 + 0.1 * jax.random.normal(key_of[8], (H,), jnp.float32), 0.5, 1.5)
    output_norm_bias = centred(key_of[9], (H,), 0.3, 1.5, (), jnp.float32)
    return {"pair": pair, "pair_grad": pair_grad, "token_mask": token_mask, "w_edges": w_edges, "w_gate": w_gate, "w_out": w_out, "in_gain": in_gain, "in_bias": in_bias, "output_norm_gain": output_norm_gain, "output_norm_bias": output_norm_bias}


EPS = 1e-05

def apply_layer_norm(values, reduce_dimension):
    mean = lax.optimization_barrier(jnp.mean(values, axis=reduce_dimension, keepdims=True))
    var = lax.optimization_barrier(jnp.mean((values - mean) ** 2, axis=reduce_dimension, keepdims=True))
    rstd = lax.rsqrt(var + EPS)
    return ((values - mean) * rstd, rstd)

def layer_norm_backward(dnorm, gain, normed, rstd, reduce_dimension):
    scaled = dnorm * gain
    return (scaled - lax.optimization_barrier(jnp.mean(scaled, axis=reduce_dimension, keepdims=True)) - normed * lax.optimization_barrier(jnp.mean(scaled * normed, axis=reduce_dimension, keepdims=True))) * rstd

def flat_dot(left_arr, right_arr):
    return jnp.dot(left_arr.reshape(-1, left_arr.shape[-1]), right_arr, preferred_element_type=jnp.float32).reshape(left_arr.shape[:-1] + (right_arr.shape[-1],))

def outer_sum(left_arr, right_arr):
    return jnp.dot(left_arr.reshape(-1, left_arr.shape[-1]).T, right_arr.reshape(-1, right_arr.shape[-1]), preferred_element_type=jnp.float32)

def one_structure(z, dout, mask, w_edges, w_gate, w_out, in_gain, in_bias, output_norm_gain, output_norm_bias):
    zhat, rstd_in = apply_layer_norm(z.astype(jnp.float32), -1)
    zn = (zhat * in_gain + in_bias).astype(jnp.bfloat16)
    maskf = mask.astype(jnp.float32)
    pm = (maskf[:, None] * maskf[None, :])[..., None]
    side_a = flat_dot(zn, w_edges[:, :2 * H])
    side_b = flat_dot(zn, w_edges[:, 2 * H:])
    sa = jax.nn.sigmoid(side_a[..., :H])
    sb = jax.nn.sigmoid(side_b[..., :H])
    left = (pm * sa * side_a[..., H:]).astype(jnp.bfloat16)
    right = (pm * sb * side_b[..., H:]).astype(jnp.bfloat16)
    triangle_product = jnp.einsum('ikh,jkh->ijh', left.astype(jnp.float32), right.astype(jnp.float32)).astype(jnp.bfloat16)
    centered_scaled_input, output_inverse_deviation = apply_layer_norm(triangle_product.astype(jnp.float32), -1)
    normalized_product = (centered_scaled_input * output_norm_gain + output_norm_bias).astype(jnp.bfloat16)
    gate = jax.nn.sigmoid(flat_dot(zn, w_gate))
    y_out = flat_dot(normalized_product, w_out)
    doutf = dout.astype(jnp.float32)
    dy = (doutf * gate).astype(jnp.bfloat16)
    dgl = (doutf * y_out * gate * (1.0 - gate)).astype(jnp.bfloat16)
    grad_out = outer_sum(normalized_product, dy)
    normalized_gradient = flat_dot(dy, w_out.T)
    output_norm_param_grads = jnp.stack([lax.optimization_barrier(jnp.sum(normalized_gradient * centered_scaled_input, axis=(0, 1))), lax.optimization_barrier(jnp.sum(normalized_gradient, axis=(0, 1)))])
    product_gradient = layer_norm_backward(normalized_gradient, output_norm_gain, centered_scaled_input, output_inverse_deviation, -1).astype(jnp.bfloat16)
    dleft = jnp.einsum('ijh,jkh->ikh', product_gradient.astype(jnp.float32), right.astype(jnp.float32)).astype(jnp.bfloat16)
    dright = jnp.einsum('ijh,ikh->jkh', product_gradient.astype(jnp.float32), left.astype(jnp.float32)).astype(jnp.bfloat16)
    dla = dleft.astype(jnp.float32) * pm
    dlb = dright.astype(jnp.float32) * pm
    dp_all = jnp.concatenate([dla * side_a[..., H:] * sa * (1.0 - sa), dla * sa, dlb * side_b[..., H:] * sb * (1.0 - sb), dlb * sb], axis=-1).astype(jnp.bfloat16)
    grad_edges = outer_sum(zn, dp_all)
    grad_gate = outer_sum(zn, dgl)
    dzn = flat_dot(dp_all, w_edges.T) + flat_dot(dgl, w_gate.T)
    grad_in_norm = jnp.stack([lax.optimization_barrier(jnp.sum(dzn * zhat, axis=(0, 1))), lax.optimization_barrier(jnp.sum(dzn, axis=(0, 1)))])
    dz = layer_norm_backward(dzn, in_gain, zhat, rstd_in, -1).astype(jnp.bfloat16)
    return (dz, (grad_edges, grad_gate, grad_out, grad_in_norm, output_norm_param_grads))

def reference(pair, pair_grad, token_mask, w_edges, w_gate, w_out, in_gain, in_bias, output_norm_gain, output_norm_bias):

    def step(carry, items):
        z, dout, mask = items
        dz, grads = one_structure(z, dout, mask, w_edges, w_gate, w_out, in_gain, in_bias, output_norm_gain, output_norm_bias)
        return (jax.tree.map(lambda total, part: total + part, carry, grads), dz)
    init = (jnp.zeros((C, 4 * H), jnp.float32), jnp.zeros((C, C), jnp.float32), jnp.zeros((H, C), jnp.float32), jnp.zeros((2, C), jnp.float32), jnp.zeros((2, H), jnp.float32))
    totals, pair_input_grad = lax.scan(step, init, (pair, pair_grad, token_mask))
    return (pair_input_grad, totals[0], totals[1], totals[2], totals[3], totals[4])
```

```python
import functools

import jax
import jax.numpy as jnp
from jax import lax
from jax.experimental import pallas as pl
from jax.experimental.pallas import tpu as pltpu
from jax.sharding import PartitionSpec as P

EPS = 1e-05
LANES = 128
F32 = jnp.float32
BF16 = jnp.bfloat16


def apply_layer_norm(values, reduce_dimension):
    mean = jnp.mean(values, axis=reduce_dimension, keepdims=True)
    var = jnp.mean((values - mean) ** 2, axis=reduce_dimension, keepdims=True)
    rstd = lax.rsqrt(var + EPS)
    return ((values - mean) * rstd, rstd)


def layer_norm_backward(dnorm, gain, normed, rstd, reduce_dimension):
    scaled = dnorm * gain
    return (
        scaled
        - jnp.mean(scaled, axis=reduce_dimension, keepdims=True)
        - normed * jnp.mean(scaled * normed, axis=reduce_dimension, keepdims=True)
    ) * rstd


def per_device_exchange(
    pair,
    pair_grad,
    token_mask,
    w_edges,
    w_gate,
    w_out,
    in_gain,
    in_bias,
    output_norm_gain,
    output_norm_bias,
):
    z_rows = pair[0]
    dout = pair_grad[0]
    rows = z_rows.shape[0]
    hidden = w_out.shape[0]
    width = w_gate.shape[0]
    first = lax.axis_index("dap") * rows
    mask_full = token_mask[0].astype(jnp.float32)
    mask_rows = lax.dynamic_slice_in_dim(mask_full, first, rows, 0)
    edge_mask = mask_rows[:, None, None] * mask_full[None, None, :]
    zhat, rstd_in = apply_layer_norm(z_rows.astype(jnp.float32), 2)
    zn = (zhat * in_gain + in_bias).astype(jnp.bfloat16)

    def project(columns):
        return jnp.einsum("ikc,ch->ihk", zn, columns, preferred_element_type=jnp.float32)

    def edge_values(pre):
        return (edge_mask * jax.nn.sigmoid(pre[:, :hidden]) * pre[:, hidden:]).astype(jnp.bfloat16)

    pre_left = project(w_edges[:, : 2 * hidden])
    pre_right = project(w_edges[:, 2 * hidden :])
    left_ch, right_ch = (
        lax.all_to_all(edge_values(pre_left), "dap", split_axis=1, concat_axis=0, tiled=True),
        lax.all_to_all(edge_values(pre_right), "dap", split_axis=1, concat_axis=0, tiled=True),
    )
    tri = jnp.einsum("ihk,jhk->ihj", left_ch, right_ch, preferred_element_type=jnp.float32).astype(
        jnp.bfloat16
    )
    triangle_product = lax.all_to_all(tri, "dap", split_axis=0, concat_axis=1, tiled=True)
    centered_scaled_input, output_inverse_deviation = apply_layer_norm(
        triangle_product.astype(jnp.float32), 1
    )
    normalized_product = (
        centered_scaled_input * output_norm_gain[None, :, None] + output_norm_bias[None, :, None]
    ).astype(jnp.bfloat16)
    gate = jax.nn.sigmoid(jnp.einsum("ijc,cd->ijd", zn, w_gate, preferred_element_type=jnp.float32))
    y_out = jnp.einsum("ihj,hc->ijc", normalized_product, w_out, preferred_element_type=jnp.float32)
    doutf = dout.astype(jnp.float32)
    dy = (doutf * gate).astype(jnp.bfloat16)
    dgl = (doutf * y_out * gate * (1.0 - gate)).astype(jnp.bfloat16)
    grad_out = jnp.einsum("ihj,ijc->hc", normalized_product, dy, preferred_element_type=jnp.float32)
    normalized_gradient = jnp.einsum("ijc,hc->ihj", dy, w_out, preferred_element_type=jnp.float32)
    output_norm_backward = jnp.stack(
        [
            jnp.sum(normalized_gradient * centered_scaled_input, axis=(0, 2)),
            jnp.sum(normalized_gradient, axis=(0, 2)),
        ]
    )
    product_gradient = layer_norm_backward(
        normalized_gradient,
        output_norm_gain[None, :, None],
        centered_scaled_input,
        output_inverse_deviation,
        1,
    ).astype(jnp.bfloat16)
    dprod_ch = lax.all_to_all(product_gradient, "dap", split_axis=1, concat_axis=0, tiled=True)
    dleft_ch = jnp.einsum(
        "ihj,jhk->ihk", dprod_ch, right_ch, preferred_element_type=jnp.float32
    ).astype(jnp.bfloat16)
    dright_ch = jnp.einsum(
        "ihj,ihk->jhk", dprod_ch, left_ch, preferred_element_type=jnp.float32
    ).astype(jnp.bfloat16)
    dleft, dright = (
        lax.all_to_all(dleft_ch, "dap", split_axis=0, concat_axis=1, tiled=True),
        lax.all_to_all(dright_ch, "dap", split_axis=0, concat_axis=1, tiled=True),
    )

    def pre_grad(dvalues, pre):
        sig = jax.nn.sigmoid(pre[:, :hidden])
        masked = dvalues.astype(jnp.float32) * edge_mask
        return jnp.concatenate(
            [masked * pre[:, hidden:] * sig * (1.0 - sig), masked * sig], axis=1
        ).astype(jnp.bfloat16)

    dpre_left = pre_grad(dleft, pre_left)
    dpre_right = pre_grad(dright, pre_right)
    grad_edges = jnp.concatenate(
        [
            jnp.einsum("ikc,ihk->ch", zn, dpre_left, preferred_element_type=jnp.float32),
            jnp.einsum("ikc,ihk->ch", zn, dpre_right, preferred_element_type=jnp.float32),
        ],
        axis=1,
    )
    grad_gate = jnp.einsum("ijc,ijd->cd", zn, dgl, preferred_element_type=jnp.float32)
    dzn = jnp.einsum(
        "ihk,ch->ikc", dpre_left, w_edges[:, : 2 * hidden], preferred_element_type=jnp.float32
    )
    dzn = dzn + jnp.einsum(
        "ihk,ch->ikc", dpre_right, w_edges[:, 2 * hidden :], preferred_element_type=jnp.float32
    )
    dzn = dzn + jnp.einsum("ijd,cd->ijc", dgl, w_gate, preferred_element_type=jnp.float32)
    in_norm_grad = jnp.stack([jnp.sum(dzn * zhat, axis=(0, 1)), jnp.sum(dzn, axis=(0, 1))])
    dz = layer_norm_backward(dzn, in_gain, zhat, rstd_in, 2).astype(jnp.bfloat16)
    flat = jnp.concatenate(
        [
            grad_edges.ravel(),
            grad_gate.ravel(),
            grad_out.ravel(),
            in_norm_grad.ravel(),
            output_norm_backward.ravel(),
        ]
    )
    summed = lax.psum(flat, ("dp", "dap"))
    edge_size = width * 4 * hidden
    gate_size = width * width
    out_size = hidden * width
    offset = 0
    total_edges = summed[offset : offset + edge_size].reshape(width, 4 * hidden)
    offset = offset + edge_size
    total_gate = summed[offset : offset + gate_size].reshape(width, width)
    offset = offset + gate_size
    total_out = summed[offset : offset + out_size].reshape(hidden, width)
    offset = offset + out_size
    total_in_norm = summed[offset : offset + 2 * width].reshape(2, width)
    offset = offset + 2 * width
    total_out_norm = summed[offset : offset + 2 * hidden].reshape(2, hidden)
    return (dz[None], total_edges, total_gate, total_out, total_in_norm, total_out_norm)


def dot(a, b):
    return jnp.dot(a, b, preferred_element_type=F32)


def dot_nt(a, b):
    return lax.dot_general(a, b, (((1,), (1,)), ((), ())), preferred_element_type=F32)


def norm_columns(x):
    mean = jnp.mean(x, axis=0, keepdims=True)
    centred = x - mean
    var = jnp.mean(centred * centred, axis=0, keepdims=True)
    rstd = lax.rsqrt(var + EPS)
    return centred * rstd, rstd


def norm_columns_backward(dnorm, gain, normed, rstd):
    scaled = dnorm * gain
    m1 = jnp.mean(scaled, axis=0, keepdims=True)
    m2 = jnp.mean(scaled * normed, axis=0, keepdims=True)
    return (scaled - m1 - normed * m2) * rstd


def block_diagonal(tiles, low):
    turned = pltpu.roll(tiles, LANES // 2, 1)
    zero = jnp.zeros((8, LANES), F32)
    top, bottom = [], []
    for a in range(tiles.shape[0] // 8):
        x = tiles[8 * a : 8 * a + 8]
        y = turned[8 * a : 8 * a + 8]
        top += [jnp.where(low, x, zero), jnp.where(low, y, zero)]
        bottom += [jnp.where(low, zero, y), jnp.where(low, zero, x)]
    return jnp.concatenate(top + bottom, axis=0).astype(BF16)


def fused_kernel(
    n_blocks,
    me_ref,
    mask_ref,
    *refs,
):
    pair_refs = refs[:n_blocks]
    pg_ref = refs[n_blocks]
    pgt_refs = refs[n_blocks + 1 : 2 * n_blocks + 1]
    (
        we_ref,
        wg_ref,
        wo_ref,
        gain_ref,
        bias_ref,
        ogain_ref,
        obias_ref,
        dz_ref,
        grads_ref,
        weT,
        wgT,
        woT,
        vec,
        pm,
        xall,
        pgs,
        ls,
        rs,
        pre_own,
        zn_own,
        zhat_own,
        rstd_own,
        bdl,
        bdr,
        pr,
        dgl_own,
        gacc,
    ) = refs[2 * n_blocks + 1 :]
    me = me_ref[0]
    rows, tokens, width = pair_refs[0].shape
    half = rows // 2
    tiles = n_blocks * half
    hidden = wo_ref.shape[0]
    f = lambda v: v.astype(F32)

    for b in range(4):
        cols = slice(b * hidden, (b + 1) * hidden)
        weT[cols, :] = f(we_ref[:, cols]).T.astype(BF16)
    wgT[...] = f(wg_ref[...]).T.astype(BF16)
    woT[...] = f(wo_ref[...]).T.astype(BF16)
    for b, r in enumerate((gain_ref, bias_ref, ogain_ref, obias_ref)):
        vec[b] = jnp.broadcast_to(r[...], (width, LANES)).T
    low = lax.broadcasted_iota(jnp.int32, (8, LANES), 1) < LANES // 2
    m = f(mask_ref[...])
    m = jnp.broadcast_to(jnp.concatenate([m, m], axis=1), (LANES, LANES))
    mt = m.T
    for a in range(n_blocks):
        lo = mt[rows * a : rows * a + half]
        hi = mt[rows * a + half : rows * (a + 1)]
        pm[half * a : half * (a + 1), :] = jnp.where(low, lo, hi) * m[:8]
    gacc[...] = jnp.zeros_like(gacc)

    for s in range(n_blocks):
        a = jnp.bitwise_xor(me, s)

        @pl.loop(0, half)
        def _(t, s=s, a=a):
            lo = f(pair_refs[s][t])
            hi = f(pair_refs[s][t + half])
            at = pl.multiple_of((a * rows + t) * tokens, tokens)
            xall[pl.ds(at, tokens), :] = lo
            xall[pl.ds(at + half * tokens, tokens), :] = hi
            zhat, rstd = norm_columns(jnp.concatenate([lo, hi], axis=0).T)
            zn = (zhat * vec[0] + vec[1]).astype(BF16)
            pre = dot(weT[...], zn)
            mask = pm[pl.ds(a * half + t, 1), :]
            left = mask * jax.nn.sigmoid(pre[:hidden]) * pre[hidden : 2 * hidden]
            right = mask * jax.nn.sigmoid(pre[2 * hidden : 3 * hidden]) * pre[3 * hidden :]
            ls[pl.ds(a * half + t, hidden, stride=tiles), :] = left
            rs[pl.ds(a * half + t, hidden, stride=tiles), :] = right
            if s == 0:
                pre_own[t] = pre
                zn_own[t] = zn
                zhat_own[t] = zhat
                rstd_own[t] = rstd

        pgs[pl.ds(pl.multiple_of(a * rows * rows, rows), rows * rows), :] = f(
            pgt_refs[s][...].reshape(rows * rows, width)
        )

    @pl.loop(0, hidden, unroll=4)
    def _(h):
        at = pl.multiple_of(h * tiles, tiles)
        own = pl.multiple_of(h * tiles + me * half, half)
        right = block_diagonal(rs[pl.ds(at, tiles), :], low)
        left = block_diagonal(ls[pl.ds(at, tiles), :], low)
        bdr[h] = right
        bdl[h] = left
        out = pl.multiple_of(h * half, half)
        pr[0, pl.ds(out, half), :] = dot_nt(ls[pl.ds(own, half), :].astype(BF16), right)
        pr[1, pl.ds(out, half), :] = dot_nt(rs[pl.ds(own, half), :].astype(BF16), left)

    @pl.loop(0, half)
    def _(t):
        for own in (True, False):
            which = 0 if own else 1
            prod = pr[which, pl.ds(t, hidden, stride=half), :].astype(BF16).astype(F32)
            xhat, rstd = norm_columns(prod)
            if own:
                zn = zn_own[t]
                pg = jnp.concatenate([f(pg_ref[t]), f(pg_ref[t + half])], axis=0).T
            else:
                j = me * rows + t
                x = jnp.concatenate(
                    [
                        xall[pl.ds(j, tokens, stride=tokens), :],
                        xall[pl.ds(j + half, tokens, stride=tokens), :],
                    ],
                    axis=0,
                ).T
                zhat, _ = norm_columns(x)
                zn = (zhat * vec[0] + vec[1]).astype(BF16)
                pg = jnp.concatenate(
                    [
                        pgs[pl.ds(t, tokens, stride=rows), :],
                        pgs[pl.ds(t + half, tokens, stride=rows), :],
                    ],
                    axis=0,
                ).T
            gate = jax.nn.sigmoid(dot(wgT[...], zn))
            dy = (pg * gate).astype(BF16)
            dxn = dot(wo_ref[...], dy)
            if own:
                xn = (xhat * vec[2] + vec[3]).astype(BF16)
                y = dot(woT[...], xn)
                dgl = (pg * y * gate * (1.0 - gate)).astype(BF16)
                dgl_own[t] = dgl
                gacc[4] += dot_nt(zn, dgl)
                gacc[5] += dot_nt(xn, dy)
                gacc[6] += dxn * xhat
                gacc[7] += dxn
            pr[which, pl.ds(t, hidden, stride=half), :] = norm_columns_backward(
                dxn, vec[2], xhat, rstd
            )

    @pl.loop(0, hidden, unroll=4)
    def _(h):
        at = pl.multiple_of(h * half, half)
        pr[0, pl.ds(at, half), :] = dot(pr[0, pl.ds(at, half), :].astype(BF16), bdr[h])
        pr[1, pl.ds(at, half), :] = dot(pr[1, pl.ds(at, half), :].astype(BF16), bdl[h])

    @pl.loop(0, half)
    def _(t):
        mask = pm[pl.ds(me * half + t, 1), :]
        zn = zn_own[t]
        zhat = zhat_own[t]
        dzn = dot(wg_ref[...], dgl_own[t])
        for which in range(2):
            d = pr[which, pl.ds(t, hidden, stride=half), :].astype(BF16).astype(F32) * mask
            sig = jax.nn.sigmoid(pre_own[t, pl.ds(2 * which * hidden, hidden), :])
            val = pre_own[t, pl.ds((2 * which + 1) * hidden, hidden), :]
            dval = d * sig
            dgate = (dval * val * (1.0 - sig)).astype(BF16)
            dval = dval.astype(BF16)
            gacc[2 * which] += dot_nt(zn, dgate)
            gacc[2 * which + 1] += dot_nt(zn, dval)
            dzn += dot(we_ref[:, 2 * which * hidden : (2 * which + 1) * hidden], dgate)
            dzn += dot(we_ref[:, (2 * which + 1) * hidden : (2 * which + 2) * hidden], dval)
        gacc[8] += dzn * zhat
        gacc[9] += dzn
        dz = norm_columns_backward(dzn, vec[0], zhat, rstd_own[t]).T.astype(BF16)
        dz_ref[t] = dz[:tokens]
        dz_ref[t + half] = dz[tokens:]

    for b in range(6):
        grads_ref[b * LANES : (b + 1) * LANES, :] = gacc[b].astype(BF16)
    sums = [jnp.sum(gacc[b].T, axis=0, keepdims=True) for b in (8, 9, 6, 7)]
    pad = grads_ref.shape[0] - 6 * LANES
    sums.append(jnp.zeros((pad - 4, LANES), F32))
    grads_ref[6 * LANES :, :] = jnp.concatenate(sums, axis=0).astype(BF16)


def pick(x, i):
    return lax.dynamic_index_in_dim(x, i, 0, keepdims=False)


def swap(x, axis, n, bit):
    return lax.ppermute(x, axis, [(i, i ^ bit) for i in range(n)])


def bits_of(n):
    out = []
    b = n // 2
    while b:
        out.append(b)
        b //= 2
    return out


def per_device_fused(
    n_dp,
    n_dap,
    pair,
    pair_grad,
    token_mask,
    w_edges,
    w_gate,
    w_out,
    in_gain,
    in_bias,
    output_norm_gain,
    output_norm_bias,
):
    rows, tokens, width = pair.shape[1:]
    hidden = w_out.shape[0]
    me = lax.axis_index("dap")
    x = pair[0]
    g = pair_grad[0]

    blocks = {0: x}
    for bit in bits_of(n_dap):
        blocks.update({s ^ bit: swap(b, "dap", n_dap, bit) for s, b in list(blocks.items())})
    cut = g.reshape(rows, n_dap, rows, width)
    parts = {
        0: {r: lax.dynamic_index_in_dim(cut, me ^ r, 1, keepdims=False) for r in range(n_dap)}
    }
    for bit in bits_of(n_dap):
        new = {}
        for s, cols in parts.items():
            new[s ^ bit] = {
                r: swap(cols[r ^ bit], "dap", n_dap, bit) for r in cols if not r & bit
            }
        parts = {s: {r: v for r, v in cols.items() if not r & bit} for s, cols in parts.items()}
        parts.update(new)
    blocks = [blocks[s] for s in range(n_dap)]
    columns = [parts[s][0] for s in range(n_dap)]

    half = rows // 2
    tiles = n_dap * half
    grad_rows = 6 * LANES + 16 * n_dap
    vm = functools.partial(pltpu.VMEM)
    dz, grads = pl.pallas_call(
        functools.partial(fused_kernel, n_dap),
        out_shape=(
            jax.ShapeDtypeStruct((rows, tokens, width), BF16),
            jax.ShapeDtypeStruct((grad_rows, LANES), BF16),
        ),
        in_specs=[pl.BlockSpec(memory_space=pltpu.SMEM)]
        + [pl.BlockSpec(memory_space=pltpu.VMEM)] * (2 * n_dap + 9),
        out_specs=(
            pl.BlockSpec(memory_space=pltpu.VMEM),
            pl.BlockSpec(memory_space=pltpu.VMEM),
        ),
        scratch_shapes=[
            vm((4 * hidden, width), BF16),
            vm((width, width), BF16),
            vm((width, hidden), BF16),
            vm((4, width, LANES), F32),
            vm((tiles, LANES), F32),
            vm((n_dap * rows * tokens, width), F32),
            vm((n_dap * rows * rows, width), F32),
            vm((hidden * tiles, LANES), F32),
            vm((hidden * tiles, LANES), F32),
            vm((half, 4 * hidden, LANES), F32),
            vm((half, width, LANES), BF16),
            vm((half, width, LANES), F32),
            vm((half, 1, LANES), F32),
            vm((hidden, LANES, LANES), BF16),
            vm((hidden, LANES, LANES), BF16),
            vm((2, hidden * half, LANES), F32),
            vm((half, width, LANES), BF16),
            vm((10, LANES, LANES), F32),
        ],
        compiler_params=pltpu.CompilerParams(vmem_limit_bytes=48 * 1024 * 1024),
    )(
        me.astype(jnp.int32).reshape(1),
        token_mask,
        *blocks,
        g,
        *columns,
        w_edges,
        w_gate,
        w_out,
        in_gain.reshape(1, -1),
        in_bias.reshape(1, -1),
        output_norm_gain.reshape(1, -1),
        output_norm_bias.reshape(1, -1),
    )

    total = grads
    for bit in reversed(bits_of(n_dap)):
        total = total.reshape(2, -1, LANES)
        mine = ((me & bit) > 0).astype(jnp.int32)
        got = swap(pick(total, 1 - mine), "dap", n_dap, bit)
        total = (pick(total, mine).astype(F32) + got.astype(F32)).astype(BF16)
    for bit in reversed(bits_of(n_dp)):
        total = (total.astype(F32) + swap(total, "dp", n_dp, bit).astype(F32)).astype(BF16)
    for bit in bits_of(n_dap):
        got = swap(total, "dap", n_dap, bit)
        first = (me & bit) == 0
        total = jnp.where(
            first, jnp.concatenate([total, got]), jnp.concatenate([got, total])
        )
    total = total.astype(F32)
    edges = total[: 4 * LANES].reshape(4, width, hidden).transpose(1, 0, 2).reshape(width, -1)
    tail = total[6 * LANES :]
    return (
        dz[None],
        edges,
        total[4 * LANES : 5 * LANES],
        total[5 * LANES : 6 * LANES],
        tail[0:2],
        tail[2:4],
    )


def solution(mesh):
    in_specs = (
        P("dp", "dap", None, None),
        P("dp", "dap", None, None),
        P("dp", None),
        P(),
        P(),
        P(),
        P(),
        P(),
        P(),
        P(),
    )
    out_specs = (P("dp", "dap", None, None), P(), P(), P(), P(), P())
    n_dp, n_dap = mesh.shape["dp"], mesh.shape["dap"]

    def per_device(pair, *others):
        structs, rows, tokens, width = pair.shape
        hidden = others[4].shape[0]
        fits = (
            structs == 1
            and 2 * tokens == LANES
            and rows == 16
            and width == LANES
            and hidden == LANES
            and n_dap & (n_dap - 1) == 0
            and n_dp & (n_dp - 1) == 0
        )
        if fits:
            return per_device_fused(n_dp, n_dap, pair, *others)
        return per_device_exchange(pair, *others)

    return jax.shard_map(
        per_device, mesh=mesh, in_specs=in_specs, out_specs=out_specs, check_vma=False
    )
```

```python
import functools

import jax
import jax.numpy as jnp
from jax import lax
from jax.experimental import pallas as pl
from jax.experimental.pallas import tpu as pltpu
from jax.sharding import PartitionSpec as P

EPS = 1e-05
LANES = 128
F32 = jnp.float32
BF16 = jnp.bfloat16


def apply_layer_norm(values, reduce_dimension):
    mean = jnp.mean(values, axis=reduce_dimension, keepdims=True)
    var = jnp.mean((values - mean) ** 2, axis=reduce_dimension, keepdims=True)
    rstd = lax.rsqrt(var + EPS)
    return ((values - mean) * rstd, rstd)


def layer_norm_backward(dnorm, gain, normed, rstd, reduce_dimension):
    scaled = dnorm * gain
    return (
        scaled
        - jnp.mean(scaled, axis=reduce_dimension, keepdims=True)
        - normed * jnp.mean(scaled * normed, axis=reduce_dimension, keepdims=True)
    ) * rstd


def per_device_exchange(
    pair,
    pair_grad,
    token_mask,
    w_edges,
    w_gate,
    w_out,
    in_gain,
    in_bias,
    output_norm_gain,
    output_norm_bias,
):
    z_rows = pair[0]
    dout = pair_grad[0]
    rows = z_rows.shape[0]
    hidden = w_out.shape[0]
    width = w_gate.shape[0]
    first = lax.axis_index("dap") * rows
    mask_full = token_mask[0].astype(jnp.float32)
    mask_rows = lax.dynamic_slice_in_dim(mask_full, first, rows, 0)
    edge_mask = mask_rows[:, None, None] * mask_full[None, None, :]
    zhat, rstd_in = apply_layer_norm(z_rows.astype(jnp.float32), 2)
    zn = (zhat * in_gain + in_bias).astype(jnp.bfloat16)

    def project(columns):
        return jnp.einsum("ikc,ch->ihk", zn, columns, preferred_element_type=jnp.float32)

    def edge_values(pre):
        return (edge_mask * jax.nn.sigmoid(pre[:, :hidden]) * pre[:, hidden:]).astype(jnp.bfloat16)

    pre_left = project(w_edges[:, : 2 * hidden])
    pre_right = project(w_edges[:, 2 * hidden :])
    left_ch, right_ch = (
        lax.all_to_all(edge_values(pre_left), "dap", split_axis=1, concat_axis=0, tiled=True),
        lax.all_to_all(edge_values(pre_right), "dap", split_axis=1, concat_axis=0, tiled=True),
    )
    tri = jnp.einsum("ihk,jhk->ihj", left_ch, right_ch, preferred_element_type=jnp.float32).astype(
        jnp.bfloat16
    )
    triangle_product = lax.all_to_all(tri, "dap", split_axis=0, concat_axis=1, tiled=True)
    centered_scaled_input, output_inverse_deviation = apply_layer_norm(
        triangle_product.astype(jnp.float32), 1
    )
    normalized_product = (
        centered_scaled_input * output_norm_gain[None, :, None] + output_norm_bias[None, :, None]
    ).astype(jnp.bfloat16)
    gate = jax.nn.sigmoid(jnp.einsum("ijc,cd->ijd", zn, w_gate, preferred_element_type=jnp.float32))
    y_out = jnp.einsum("ihj,hc->ijc", normalized_product, w_out, preferred_element_type=jnp.float32)
    doutf = dout.astype(jnp.float32)
    dy = (doutf * gate).astype(jnp.bfloat16)
    dgl = (doutf * y_out * gate * (1.0 - gate)).astype(jnp.bfloat16)
    grad_out = jnp.einsum("ihj,ijc->hc", normalized_product, dy, preferred_element_type=jnp.float32)
    normalized_gradient = jnp.einsum("ijc,hc->ihj", dy, w_out, preferred_element_type=jnp.float32)
    output_norm_backward = jnp.stack(
        [
            jnp.sum(normalized_gradient * centered_scaled_input, axis=(0, 2)),
            jnp.sum(normalized_gradient, axis=(0, 2)),
        ]
    )
    product_gradient = layer_norm_backward(
        normalized_gradient,
        output_norm_gain[None, :, None],
        centered_scaled_input,
        output_inverse_deviation,
        1,
    ).astype(jnp.bfloat16)
    dprod_ch = lax.all_to_all(product_gradient, "dap", split_axis=1, concat_axis=0, tiled=True)
    dleft_ch = jnp.einsum(
        "ihj,jhk->ihk", dprod_ch, right_ch, preferred_element_type=jnp.float32
    ).astype(jnp.bfloat16)
    dright_ch = jnp.einsum(
        "ihj,ihk->jhk", dprod_ch, left_ch, preferred_element_type=jnp.float32
    ).astype(jnp.bfloat16)
    dleft, dright = (
        lax.all_to_all(dleft_ch, "dap", split_axis=0, concat_axis=1, tiled=True),
        lax.all_to_all(dright_ch, "dap", split_axis=0, concat_axis=1, tiled=True),
    )

    def pre_grad(dvalues, pre):
        sig = jax.nn.sigmoid(pre[:, :hidden])
        masked = dvalues.astype(jnp.float32) * edge_mask
        return jnp.concatenate(
            [masked * pre[:, hidden:] * sig * (1.0 - sig), masked * sig], axis=1
        ).astype(jnp.bfloat16)

    dpre_left = pre_grad(dleft, pre_left)
    dpre_right = pre_grad(dright, pre_right)
    grad_edges = jnp.concatenate(
        [
            jnp.einsum("ikc,ihk->ch", zn, dpre_left, preferred_element_type=jnp.float32),
            jnp.einsum("ikc,ihk->ch", zn, dpre_right, preferred_element_type=jnp.float32),
        ],
        axis=1,
    )
    grad_gate = jnp.einsum("ijc,ijd->cd", zn, dgl, preferred_element_type=jnp.float32)
    dzn = jnp.einsum(
        "ihk,ch->ikc", dpre_left, w_edges[:, : 2 * hidden], preferred_element_type=jnp.float32
    )
    dzn = dzn + jnp.einsum(
        "ihk,ch->ikc", dpre_right, w_edges[:, 2 * hidden :], preferred_element_type=jnp.float32
    )
    dzn = dzn + jnp.einsum("ijd,cd->ijc", dgl, w_gate, preferred_element_type=jnp.float32)
    in_norm_grad = jnp.stack([jnp.sum(dzn * zhat, axis=(0, 1)), jnp.sum(dzn, axis=(0, 1))])
    dz = layer_norm_backward(dzn, in_gain, zhat, rstd_in, 2).astype(jnp.bfloat16)
    flat = jnp.concatenate(
        [
            grad_edges.ravel(),
            grad_gate.ravel(),
            grad_out.ravel(),
            in_norm_grad.ravel(),
            output_norm_backward.ravel(),
        ]
    )
    summed = lax.psum(flat, ("dp", "dap"))
    edge_size = width * 4 * hidden
    gate_size = width * width
    out_size = hidden * width
    offset = 0
    total_edges = summed[offset : offset + edge_size].reshape(width, 4 * hidden)
    offset = offset + edge_size
    total_gate = summed[offset : offset + gate_size].reshape(width, width)
    offset = offset + gate_size
    total_out = summed[offset : offset + out_size].reshape(hidden, width)
    offset = offset + out_size
    total_in_norm = summed[offset : offset + 2 * width].reshape(2, width)
    offset = offset + 2 * width
    total_out_norm = summed[offset : offset + 2 * hidden].reshape(2, hidden)
    return (dz[None], total_edges, total_gate, total_out, total_in_norm, total_out_norm)


def dot(a, b):
    return jnp.dot(a, b, preferred_element_type=F32)


def dot_nt(a, b):
    return lax.dot_general(a, b, (((1,), (1,)), ((), ())), preferred_element_type=F32)


def norm_columns(x):
    mean = jnp.mean(x, axis=0, keepdims=True)
    centred = x - mean
    var = jnp.mean(centred * centred, axis=0, keepdims=True)
    rstd = lax.rsqrt(var + EPS)
    return centred * rstd, rstd


def norm_columns_backward(dnorm, gain, normed, rstd):
    scaled = dnorm * gain
    m1 = jnp.mean(scaled, axis=0, keepdims=True)
    m2 = jnp.mean(scaled * normed, axis=0, keepdims=True)
    return (scaled - m1 - normed * m2) * rstd


def halves(x):
    n = LANES // 2
    return jnp.concatenate([x[:, :n], x[:, n:]], axis=0).astype(BF16)


def lanes(x):
    return jnp.concatenate([x[:8], x[8:]], axis=1)


def square(tiles):
    n = LANES // 2
    parts = []
    for a in range(tiles.shape[0] // 8):
        x = tiles[8 * a : 8 * a + 8]
        parts += [x[:, :n], x[:, n:]]
    return jnp.concatenate(parts, axis=0).astype(BF16)


def fused_kernel(
    n_blocks,
    me_ref,
    mask_ref,
    *refs,
):
    pair_refs = refs[:n_blocks]
    pg_ref = refs[n_blocks]
    pgt_refs = refs[n_blocks + 1 : 2 * n_blocks + 1]
    (
        we_ref,
        wg_ref,
        wo_ref,
        gain_ref,
        bias_ref,
        ogain_ref,
        obias_ref,
        dz_ref,
        grads_ref,
        weT,
        wgT,
        woT,
        vec,
        pm,
        xall,
        pgs,
        ls,
        rs,
        pre_own,
        zn_own,
        zhat_own,
        rstd_own,
        bdl,
        bdr,
        pr,
        dgl_own,
        gacc,
    ) = refs[2 * n_blocks + 1 :]
    me = me_ref[0]
    rows, tokens, width = pair_refs[0].shape
    half = rows // 2
    tiles = n_blocks * half
    hidden = wo_ref.shape[0]
    f = lambda v: v.astype(F32)

    for b in range(4):
        cols = slice(b * hidden, (b + 1) * hidden)
        weT[cols, :] = f(we_ref[:, cols]).T.astype(BF16)
    wgT[...] = f(wg_ref[...]).T.astype(BF16)
    woT[...] = f(wo_ref[...]).T.astype(BF16)
    for b, r in enumerate((gain_ref, bias_ref, ogain_ref, obias_ref)):
        vec[b] = jnp.broadcast_to(r[...], (width, LANES)).T
    low = lax.broadcasted_iota(jnp.int32, (8, LANES), 1) < LANES // 2
    m = f(mask_ref[...])
    m = jnp.broadcast_to(jnp.concatenate([m, m], axis=1), (LANES, LANES))
    mt = m.T
    for a in range(n_blocks):
        lo = mt[rows * a : rows * a + half]
        hi = mt[rows * a + half : rows * (a + 1)]
        pm[half * a : half * (a + 1), :] = jnp.where(low, lo, hi) * m[:8]
    gacc[...] = jnp.zeros_like(gacc)

    for s in range(n_blocks):
        a = jnp.bitwise_xor(me, s)

        @pl.loop(0, half, unroll=8)
        def _(t, s=s, a=a):
            lo = f(pair_refs[s][t])
            hi = f(pair_refs[s][t + half])
            at = pl.multiple_of((a * rows + t) * tokens, tokens)
            xall[pl.ds(at, tokens), :] = lo
            xall[pl.ds(at + half * tokens, tokens), :] = hi
            zhat, rstd = norm_columns(jnp.concatenate([lo, hi], axis=0).T)
            zn = (zhat * vec[0] + vec[1]).astype(BF16)
            pre = dot(weT[...], zn)
            mask = pm[pl.ds(a * half + t, 1), :]
            left = mask * jax.nn.sigmoid(pre[:hidden]) * pre[hidden : 2 * hidden]
            right = mask * jax.nn.sigmoid(pre[2 * hidden : 3 * hidden]) * pre[3 * hidden :]
            ls[pl.ds(a * half + t, hidden, stride=tiles), :] = left
            rs[pl.ds(a * half + t, hidden, stride=tiles), :] = right
            if s == 0:
                pre_own[t] = pre
                zn_own[t] = zn
                zhat_own[t] = zhat
                rstd_own[t] = rstd

        pgs[pl.ds(pl.multiple_of(a * rows * rows, rows), rows * rows), :] = f(
            pgt_refs[s][...].reshape(rows * rows, width)
        )

    @pl.loop(0, hidden, unroll=32)
    def _(h):
        at = pl.multiple_of(h * tiles, tiles)
        own = pl.multiple_of(h * tiles + me * half, half)
        right = square(rs[pl.ds(at, tiles), :])
        left = square(ls[pl.ds(at, tiles), :])
        bdr[h] = right
        bdl[h] = left
        out = pl.multiple_of(h * half, half)
        pr[0, pl.ds(out, half), :] = lanes(dot_nt(halves(ls[pl.ds(own, half), :]), right))
        pr[1, pl.ds(out, half), :] = lanes(dot_nt(halves(rs[pl.ds(own, half), :]), left))

    @pl.loop(0, half, unroll=8)
    def _(t):
        for own in (True, False):
            which = 0 if own else 1
            prod = pr[which, pl.ds(t, hidden, stride=half), :].astype(BF16).astype(F32)
            xhat, rstd = norm_columns(prod)
            if own:
                zn = zn_own[t]
                pg = jnp.concatenate([f(pg_ref[t]), f(pg_ref[t + half])], axis=0).T
            else:
                j = me * rows + t
                x = jnp.concatenate(
                    [
                        xall[pl.ds(j, tokens, stride=tokens), :],
                        xall[pl.ds(j + half, tokens, stride=tokens), :],
                    ],
                    axis=0,
                ).T
                zhat, _ = norm_columns(x)
                zn = (zhat * vec[0] + vec[1]).astype(BF16)
                pg = jnp.concatenate(
                    [
                        pgs[pl.ds(t, tokens, stride=rows), :],
                        pgs[pl.ds(t + half, tokens, stride=rows), :],
                    ],
                    axis=0,
                ).T
            gate = jax.nn.sigmoid(dot(wgT[...], zn))
            dy = (pg * gate).astype(BF16)
            dxn = dot(wo_ref[...], dy)
            if own:
                xn = (xhat * vec[2] + vec[3]).astype(BF16)
                y = dot(woT[...], xn)
                dgl = (pg * y * gate * (1.0 - gate)).astype(BF16)
                dgl_own[t] = dgl
                gacc[4] += dot_nt(zn, dgl)
                gacc[5] += dot_nt(xn, dy)
                gacc[6] += dxn * xhat
                gacc[7] += dxn
            pr[which, pl.ds(t, hidden, stride=half), :] = norm_columns_backward(
                dxn, vec[2], xhat, rstd
            )

    @pl.loop(0, hidden, unroll=32)
    def _(h):
        at = pl.multiple_of(h * half, half)
        pr[0, pl.ds(at, half), :] = lanes(dot(halves(pr[0, pl.ds(at, half), :]), bdr[h]))
        pr[1, pl.ds(at, half), :] = lanes(dot(halves(pr[1, pl.ds(at, half), :]), bdl[h]))

    @pl.loop(0, half, unroll=8)
    def _(t):
        mask = pm[pl.ds(me * half + t, 1), :]
        zn = zn_own[t]
        zhat = zhat_own[t]
        dzn = dot(wg_ref[...], dgl_own[t])
        for which in range(2):
            d = pr[which, pl.ds(t, hidden, stride=half), :].astype(BF16).astype(F32) * mask
            sig = jax.nn.sigmoid(pre_own[t, pl.ds(2 * which * hidden, hidden), :])
            val = pre_own[t, pl.ds((2 * which + 1) * hidden, hidden), :]
            dval = d * sig
            dgate = (dval * val * (1.0 - sig)).astype(BF16)
            dval = dval.astype(BF16)
            gacc[2 * which] += dot_nt(zn, dgate)
            gacc[2 * which + 1] += dot_nt(zn, dval)
            dzn += dot(we_ref[:, 2 * which * hidden : (2 * which + 1) * hidden], dgate)
            dzn += dot(we_ref[:, (2 * which + 1) * hidden : (2 * which + 2) * hidden], dval)
        gacc[8] += dzn * zhat
        gacc[9] += dzn
        dz = norm_columns_backward(dzn, vec[0], zhat, rstd_own[t]).T.astype(BF16)
        dz_ref[t] = dz[:tokens]
        dz_ref[t + half] = dz[tokens:]

    total = grads_ref
    for b in range(6):
        total[b * LANES : (b + 1) * LANES, :] = gacc[b].astype(BF16)
    sums = [jnp.sum(gacc[b].T, axis=0, keepdims=True) for b in (8, 9, 6, 7)]
    pad = total.shape[0] - 6 * LANES
    sums.append(jnp.zeros((pad - 4, LANES), F32))
    total[6 * LANES :, :] = jnp.concatenate(sums, axis=0).astype(BF16)


def finish_kernel(n_blocks, me_ref, *refs):
    chunks = refs[:n_blocks]
    edges_ref, gate_ref, out_ref, in_norm_ref, out_norm_ref, total = refs[n_blocks:]
    me = me_ref[0]
    rows = chunks[0].shape[0]
    for s in range(n_blocks):
        at = pl.multiple_of(jnp.bitwise_xor(me, s) * rows, rows)
        total[pl.ds(at, rows), :] = chunks[s][...].astype(F32)
    for b in range(4):
        edges_ref[:, b * LANES : (b + 1) * LANES] = total[b * LANES : (b + 1) * LANES, :]
    gate_ref[...] = total[4 * LANES : 5 * LANES, :]
    out_ref[...] = total[5 * LANES : 6 * LANES, :]
    in_norm_ref[...] = total[6 * LANES : 6 * LANES + 2, :]
    out_norm_ref[...] = total[6 * LANES + 2 : 6 * LANES + 4, :]


def pick(x, i):
    return lax.dynamic_index_in_dim(x, i, 0, keepdims=False)


def swap(x, axis, n, bit):
    return lax.ppermute(x, axis, [(i, i ^ bit) for i in range(n)])


def bits_of(n):
    out = []
    b = n // 2
    while b:
        out.append(b)
        b //= 2
    return out


def per_device_fused(
    n_dp,
    n_dap,
    pair,
    pair_grad,
    token_mask,
    w_edges,
    w_gate,
    w_out,
    in_gain,
    in_bias,
    output_norm_gain,
    output_norm_bias,
):
    rows, tokens, width = pair.shape[1:]
    hidden = w_out.shape[0]
    me = lax.axis_index("dap")
    place = me.astype(jnp.int32).reshape(1)
    x = pair[0]
    g = pair_grad[0]

    blocks = {0: x}
    columns = {0: g}
    for bit in bits_of(n_dap):
        keep, give = {}, {}
        for s, c in columns.items():
            c = c.reshape(rows, -1, 2, bit * rows, width)
            mine = ((me & bit) > 0).astype(jnp.int32)
            keep[s] = lax.dynamic_index_in_dim(c, mine, 2, keepdims=False).reshape(rows, -1, width)
            give[s] = lax.dynamic_index_in_dim(c, 1 - mine, 2, keepdims=False).reshape(
                rows, -1, width
            )
        got = {s ^ bit: swap(b, "dap", n_dap, bit) for s, b in blocks.items()}
        got_columns = {s ^ bit: swap(c, "dap", n_dap, bit) for s, c in give.items()}
        got, got_columns = lax.optimization_barrier((got, got_columns))
        blocks.update(got)
        columns = {**keep, **got_columns}
    blocks = [blocks[s] for s in range(n_dap)]
    columns = [columns[s] for s in range(n_dap)]

    half = rows // 2
    tiles = n_dap * half
    grad_rows = 6 * LANES + 16 * n_dap
    vm = functools.partial(pltpu.VMEM)
    dz, grads = pl.pallas_call(
        functools.partial(fused_kernel, n_dap),
        out_shape=(
            jax.ShapeDtypeStruct((rows, tokens, width), BF16),
            jax.ShapeDtypeStruct((grad_rows, LANES), BF16),
        ),
        in_specs=[pl.BlockSpec(memory_space=pltpu.SMEM)]
        + [pl.BlockSpec(memory_space=pltpu.VMEM)] * (2 * n_dap + 9),
        out_specs=(
            pl.BlockSpec(memory_space=pltpu.VMEM),
            pl.BlockSpec(memory_space=pltpu.VMEM),
        ),
        scratch_shapes=[
            vm((4 * hidden, width), BF16),
            vm((width, width), BF16),
            vm((width, hidden), BF16),
            vm((4, width, LANES), F32),
            vm((tiles, LANES), F32),
            vm((n_dap * rows * tokens, width), F32),
            vm((n_dap * rows * rows, width), F32),
            vm((hidden * tiles, LANES), F32),
            vm((hidden * tiles, LANES), F32),
            vm((half, 4 * hidden, LANES), F32),
            vm((half, width, LANES), BF16),
            vm((half, width, LANES), F32),
            vm((half, 1, LANES), F32),
            vm((hidden, tokens, tokens), BF16),
            vm((hidden, tokens, tokens), BF16),
            vm((2, hidden * half, LANES), F32),
            vm((half, width, LANES), BF16),
            vm((10, LANES, LANES), F32),
        ],
        compiler_params=pltpu.CompilerParams(vmem_limit_bytes=48 * 1024 * 1024),
    )(
        place,
        token_mask,
        *blocks,
        g,
        *columns,
        w_edges,
        w_gate,
        w_out,
        in_gain.reshape(1, -1),
        in_bias.reshape(1, -1),
        output_norm_gain.reshape(1, -1),
        output_norm_bias.reshape(1, -1),
    )

    chunks = grads.reshape(n_dap, -1, LANES)
    total = pick(chunks, me).astype(F32)
    got = [swap(pick(chunks, me ^ s), "dap", n_dap, s) for s in range(1, n_dap)]
    for c in got:
        total = total + c.astype(F32)
    total = total.astype(BF16)
    bits = bits_of(n_dp)[::-1]
    for i in range(0, len(bits), 2):
        terms = [total.astype(F32)]
        shifts = [0]
        for bit in bits[i : i + 2]:
            shifts += [s ^ bit for s in shifts]
        terms += [swap(total, "dp", n_dp, s).astype(F32) for s in shifts[1:]]
        while len(terms) > 1:
            terms = [p + q for p, q in zip(terms[::2], terms[1::2])]
        total = terms[0].astype(BF16)
    parts = [total] + [swap(total, "dap", n_dap, s) for s in range(1, n_dap)]
    out = lambda *shape: jax.ShapeDtypeStruct(shape, F32)
    edges, gate, outs, in_norm, out_norm = pl.pallas_call(
        functools.partial(finish_kernel, n_dap),
        out_shape=(
            out(width, 4 * hidden),
            out(width, width),
            out(hidden, width),
            out(2, width),
            out(2, hidden),
        ),
        in_specs=[pl.BlockSpec(memory_space=pltpu.SMEM)]
        + [pl.BlockSpec(memory_space=pltpu.VMEM)] * n_dap,
        out_specs=(pl.BlockSpec(memory_space=pltpu.VMEM),) * 5,
        scratch_shapes=[vm((grad_rows, LANES), F32)],
    )(place, *parts)
    return (dz[None], edges, gate, outs, in_norm, out_norm)


def solution(mesh):
    in_specs = (
        P("dp", "dap", None, None),
        P("dp", "dap", None, None),
        P("dp", None),
        P(),
        P(),
        P(),
        P(),
        P(),
        P(),
        P(),
    )
    out_specs = (P("dp", "dap", None, None), P(), P(), P(), P(), P())
    n_dp, n_dap = mesh.shape["dp"], mesh.shape["dap"]

    def per_device(pair, *others):
        structs, rows, tokens, width = pair.shape
        hidden = others[4].shape[0]
        fits = (
            structs == 1
            and 2 * tokens == LANES
            and rows == 16
            and width == LANES
            and hidden == LANES
            and n_dap & (n_dap - 1) == 0
            and n_dp & (n_dp - 1) == 0
        )
        if fits:
            return per_device_fused(n_dp, n_dap, pair, *others)
        return per_device_exchange(pair, *others)

    return jax.shard_map(
        per_device, mesh=mesh, in_specs=in_specs, out_specs=out_specs, check_vma=False
    )
```

```python
import functools

import jax
import jax.numpy as jnp
from jax import lax
from jax.experimental import pallas as pl
from jax.experimental.pallas import tpu as pltpu
from jax.sharding import PartitionSpec as P

EPS = 1e-05
LANES = 128
VMEM_BYTES = 32 * 1024 * 1024
F32 = jnp.float32
BF16 = jnp.bfloat16


def apply_layer_norm(values, reduce_dimension):
    mean = jnp.mean(values, axis=reduce_dimension, keepdims=True)
    var = jnp.mean((values - mean) ** 2, axis=reduce_dimension, keepdims=True)
    rstd = lax.rsqrt(var + EPS)
    return ((values - mean) * rstd, rstd)


def layer_norm_backward(dnorm, gain, normed, rstd, reduce_dimension):
    scaled = dnorm * gain
    return (
        scaled
        - jnp.mean(scaled, axis=reduce_dimension, keepdims=True)
        - normed * jnp.mean(scaled * normed, axis=reduce_dimension, keepdims=True)
    ) * rstd


def per_device_exchange(
    pair,
    pair_grad,
    token_mask,
    w_edges,
    w_gate,
    w_out,
    in_gain,
    in_bias,
    output_norm_gain,
    output_norm_bias,
):
    z_rows = pair[0]
    dout = pair_grad[0]
    rows = z_rows.shape[0]
    hidden = w_out.shape[0]
    width = w_gate.shape[0]
    first = lax.axis_index("dap") * rows
    mask_full = token_mask[0].astype(jnp.float32)
    mask_rows = lax.dynamic_slice_in_dim(mask_full, first, rows, 0)
    edge_mask = mask_rows[:, None, None] * mask_full[None, None, :]
    zhat, rstd_in = apply_layer_norm(z_rows.astype(jnp.float32), 2)
    zn = (zhat * in_gain + in_bias).astype(jnp.bfloat16)

    def project(columns):
        return jnp.einsum("ikc,ch->ihk", zn, columns, preferred_element_type=jnp.float32)

    def edge_values(pre):
        return (edge_mask * jax.nn.sigmoid(pre[:, :hidden]) * pre[:, hidden:]).astype(jnp.bfloat16)

    pre_left = project(w_edges[:, : 2 * hidden])
    pre_right = project(w_edges[:, 2 * hidden :])
    left_ch, right_ch = (
        lax.all_to_all(edge_values(pre_left), "dap", split_axis=1, concat_axis=0, tiled=True),
        lax.all_to_all(edge_values(pre_right), "dap", split_axis=1, concat_axis=0, tiled=True),
    )
    tri = jnp.einsum("ihk,jhk->ihj", left_ch, right_ch, preferred_element_type=jnp.float32).astype(
        jnp.bfloat16
    )
    triangle_product = lax.all_to_all(tri, "dap", split_axis=0, concat_axis=1, tiled=True)
    centered_scaled_input, output_inverse_deviation = apply_layer_norm(
        triangle_product.astype(jnp.float32), 1
    )
    normalized_product = (
        centered_scaled_input * output_norm_gain[None, :, None] + output_norm_bias[None, :, None]
    ).astype(jnp.bfloat16)
    gate = jax.nn.sigmoid(jnp.einsum("ijc,cd->ijd", zn, w_gate, preferred_element_type=jnp.float32))
    y_out = jnp.einsum("ihj,hc->ijc", normalized_product, w_out, preferred_element_type=jnp.float32)
    doutf = dout.astype(jnp.float32)
    dy = (doutf * gate).astype(jnp.bfloat16)
    dgl = (doutf * y_out * gate * (1.0 - gate)).astype(jnp.bfloat16)
    grad_out = jnp.einsum("ihj,ijc->hc", normalized_product, dy, preferred_element_type=jnp.float32)
    normalized_gradient = jnp.einsum("ijc,hc->ihj", dy, w_out, preferred_element_type=jnp.float32)
    output_norm_backward = jnp.stack(
        [
            jnp.sum(normalized_gradient * centered_scaled_input, axis=(0, 2)),
            jnp.sum(normalized_gradient, axis=(0, 2)),
        ]
    )
    product_gradient = layer_norm_backward(
        normalized_gradient,
        output_norm_gain[None, :, None],
        centered_scaled_input,
        output_inverse_deviation,
        1,
    ).astype(jnp.bfloat16)
    dprod_ch = lax.all_to_all(product_gradient, "dap", split_axis=1, concat_axis=0, tiled=True)
    dleft_ch = jnp.einsum(
        "ihj,jhk->ihk", dprod_ch, right_ch, preferred_element_type=jnp.float32
    ).astype(jnp.bfloat16)
    dright_ch = jnp.einsum(
        "ihj,ihk->jhk", dprod_ch, left_ch, preferred_element_type=jnp.float32
    ).astype(jnp.bfloat16)
    dleft, dright = (
        lax.all_to_all(dleft_ch, "dap", split_axis=0, concat_axis=1, tiled=True),
        lax.all_to_all(dright_ch, "dap", split_axis=0, concat_axis=1, tiled=True),
    )

    def pre_grad(dvalues, pre):
        sig = jax.nn.sigmoid(pre[:, :hidden])
        masked = dvalues.astype(jnp.float32) * edge_mask
        return jnp.concatenate(
            [masked * pre[:, hidden:] * sig * (1.0 - sig), masked * sig], axis=1
        ).astype(jnp.bfloat16)

    dpre_left = pre_grad(dleft, pre_left)
    dpre_right = pre_grad(dright, pre_right)
    grad_edges = jnp.concatenate(
        [
            jnp.einsum("ikc,ihk->ch", zn, dpre_left, preferred_element_type=jnp.float32),
            jnp.einsum("ikc,ihk->ch", zn, dpre_right, preferred_element_type=jnp.float32),
        ],
        axis=1,
    )
    grad_gate = jnp.einsum("ijc,ijd->cd", zn, dgl, preferred_element_type=jnp.float32)
    dzn = jnp.einsum(
        "ihk,ch->ikc", dpre_left, w_edges[:, : 2 * hidden], preferred_element_type=jnp.float32
    )
    dzn = dzn + jnp.einsum(
        "ihk,ch->ikc", dpre_right, w_edges[:, 2 * hidden :], preferred_element_type=jnp.float32
    )
    dzn = dzn + jnp.einsum("ijd,cd->ijc", dgl, w_gate, preferred_element_type=jnp.float32)
    in_norm_grad = jnp.stack([jnp.sum(dzn * zhat, axis=(0, 1)), jnp.sum(dzn, axis=(0, 1))])
    dz = layer_norm_backward(dzn, in_gain, zhat, rstd_in, 2).astype(jnp.bfloat16)
    flat = jnp.concatenate(
        [
            grad_edges.ravel(),
            grad_gate.ravel(),
            grad_out.ravel(),
            in_norm_grad.ravel(),
            output_norm_backward.ravel(),
        ]
    )
    summed = lax.psum(flat, ("dp", "dap"))
    edge_size = width * 4 * hidden
    gate_size = width * width
    out_size = hidden * width
    offset = 0
    total_edges = summed[offset : offset + edge_size].reshape(width, 4 * hidden)
    offset = offset + edge_size
    total_gate = summed[offset : offset + gate_size].reshape(width, width)
    offset = offset + gate_size
    total_out = summed[offset : offset + out_size].reshape(hidden, width)
    offset = offset + out_size
    total_in_norm = summed[offset : offset + 2 * width].reshape(2, width)
    offset = offset + 2 * width
    total_out_norm = summed[offset : offset + 2 * hidden].reshape(2, hidden)
    return (dz[None], total_edges, total_gate, total_out, total_in_norm, total_out_norm)


def dot(a, b):
    return jnp.dot(a, b, preferred_element_type=F32)


def dot_nt(a, b):
    return lax.dot_general(a, b, (((1,), (1,)), ((), ())), preferred_element_type=F32)


def norm_columns(x):
    mean = jnp.mean(x, axis=0, keepdims=True)
    centred = x - mean
    var = jnp.mean(centred * centred, axis=0, keepdims=True)
    rstd = lax.rsqrt(var + EPS)
    return centred * rstd, rstd


def norm_columns_backward(dnorm, gain, normed, rstd):
    scaled = dnorm * gain
    m1 = jnp.mean(scaled, axis=0, keepdims=True)
    m2 = jnp.mean(scaled * normed, axis=0, keepdims=True)
    return (scaled - m1 - normed * m2) * rstd


def halves(x):
    n = LANES // 2
    return jnp.concatenate([x[:, :n], x[:, n:]], axis=0).astype(BF16)


def lanes(x):
    return jnp.concatenate([x[:8], x[8:]], axis=1)


def square(blocks):
    n = LANES // 2
    return jnp.concatenate([p for x in blocks for p in (x[:, :n], x[:, n:])], axis=0).astype(BF16)


def columns_of(ref):
    return jnp.broadcast_to(ref[...], (ref.shape[1], LANES)).T


def transposed(ref):
    return ref[...].astype(F32).T.astype(BF16)


def fill_pair_mask(mask_ref, pm, rows):
    half = rows // 2
    low = lax.broadcasted_iota(jnp.int32, (half, LANES), 1) < LANES // 2
    m = mask_ref[...].astype(F32)
    m = jnp.broadcast_to(jnp.concatenate([m, m], axis=1), (LANES, LANES))
    mt = m.T
    for a in range(pm.shape[0] // half):
        lo = mt[rows * a : rows * a + half]
        hi = mt[rows * a + half : rows * (a + 1)]
        pm[half * a : half * (a + 1), :] = jnp.where(low, lo, hi) * m[:half]


def two_rows(ref, t):
    half = ref.shape[0] // 2
    return jnp.concatenate([ref[t].astype(F32), ref[t + half].astype(F32)], axis=0).T


def edge_tile(pair_ref, t, block, place, weT, vec, pm, ls, rs):
    half = pair_ref.shape[0] // 2
    hidden = weT.shape[0] // 4
    zhat, rstd = norm_columns(two_rows(pair_ref, t))
    zn = (zhat * vec[0] + vec[1]).astype(BF16)
    pre = dot(weT[...], zn)
    mask = pm[pl.ds(block * half + t, 1), :]
    ls[place, pl.ds(t, hidden, stride=half), :] = (
        mask * jax.nn.sigmoid(pre[:hidden]) * pre[hidden : 2 * hidden]
    )
    rs[place, pl.ds(t, hidden, stride=half), :] = (
        mask * jax.nn.sigmoid(pre[2 * hidden : 3 * hidden]) * pre[3 * hidden :]
    )
    return zhat, rstd, zn, pre


def near_kernel(
    me_ref,
    near_ref,
    mask_hbm,
    own_hbm,
    we_hbm,
    gain_hbm,
    bias_hbm,
    weT,
    ls,
    rs,
    pre_own,
    zn_own,
    zhat_own,
    rstd_own,
    vec,
    pm,
    mask_ref,
    own_ref,
    we_ref,
    gain_ref,
    bias_ref,
    sems,
):
    me = me_ref[0]
    copies = [
        pltpu.make_async_copy(src, dst, sems.at[i])
        for i, (src, dst) in enumerate(
            (
                (we_hbm, we_ref),
                (own_hbm, own_ref),
                (mask_hbm, mask_ref),
                (gain_hbm, gain_ref),
                (bias_hbm, bias_ref),
            )
        )
    ]
    for copy in copies:
        copy.start()
    for copy in copies:
        copy.wait()
    rows = own_ref.shape[0]
    half = rows // 2
    hidden = we_ref.shape[1] // 4
    for b in range(4):
        cols = slice(b * hidden, (b + 1) * hidden)
        weT[cols, :] = we_ref[:, cols].astype(F32).T.astype(BF16)
    vec[0] = columns_of(gain_ref)
    vec[1] = columns_of(bias_ref)
    fill_pair_mask(mask_ref, pm, rows)
    for s, ref in enumerate((own_ref, near_ref)):
        block = jnp.bitwise_xor(me, s)
        place = jnp.bitwise_and(block, 1)

        @pl.loop(0, half, unroll=8)
        def _(t, s=s, ref=ref, block=block, place=place):
            zhat, rstd, zn, pre = edge_tile(ref, t, block, place, weT, vec, pm, ls, rs)
            if s == 0:
                pre_own[t] = pre
                zn_own[t] = zn
                zhat_own[t] = zhat
                rstd_own[t] = rstd


def product_kernel(
    me_ref,
    mask_ref,
    pair0,
    pair1,
    pair2,
    pair3,
    weT,
    near_ls,
    near_rs,
    gain_ref,
    bias_ref,
    prod,
    left_sq,
    right_sq,
    zn_cols,
    vec,
    pm,
    xall,
    far_ls,
    far_rs,
):
    me = me_ref[0]
    rows, tokens, _ = pair0.shape
    half = rows // 2
    hidden = weT.shape[0] // 4
    vec[0] = columns_of(gain_ref)
    vec[1] = columns_of(bias_ref)
    fill_pair_mask(mask_ref, pm, rows)
    for s, ref in ((2, pair2), (3, pair3)):
        block = jnp.bitwise_xor(me, s)
        place = jnp.bitwise_and(block, 1)

        @pl.loop(0, half, unroll=8)
        def _(t, ref=ref, block=block, place=place):
            edge_tile(ref, t, block, place, weT, vec, pm, far_ls, far_rs)

    for s, ref in enumerate((pair0, pair1, pair2, pair3)):
        at = pl.multiple_of(jnp.bitwise_xor(me, s) * rows * tokens, rows * tokens)
        xall[pl.ds(at, rows * tokens), :] = ref[...].reshape(rows * tokens, -1).astype(F32)

    core = jnp.bitwise_and(me, 1)
    group = me // 2
    n_near = pl.multiple_of(group * 2 * rows, 2 * rows)
    n_far = pl.multiple_of((1 - group) * 2 * rows, 2 * rows)

    @pl.loop(0, hidden, unroll=32)
    def _(h):
        at = pl.ds(pl.multiple_of(h * half, half), half)
        for near, far, sq in ((near_ls, far_ls, left_sq), (near_rs, far_rs, right_sq)):
            sq[h, pl.ds(n_near, 2 * rows), :] = square((near[0, at, :], near[1, at, :]))
            sq[h, pl.ds(n_far, 2 * rows), :] = square((far[0, at, :], far[1, at, :]))
        prod[0, at, :] = lanes(dot_nt(halves(near_ls[core, at, :]), right_sq[h]))
        prod[1, at, :] = lanes(dot_nt(halves(near_rs[core, at, :]), left_sq[h]))

    @pl.loop(0, half, unroll=8)
    def _(t):
        j = me * rows + t
        x = jnp.concatenate(
            [
                xall[pl.ds(j, tokens, stride=tokens), :],
                xall[pl.ds(j + half, tokens, stride=tokens), :],
            ],
            axis=0,
        ).T
        zhat, _ = norm_columns(x)
        zn_cols[t] = (zhat * vec[0] + vec[1]).astype(BF16)


def back_kernel(
    me_ref,
    mask_ref,
    prod,
    left_sq,
    right_sq,
    zn_cols,
    pre_own,
    zn_own,
    zhat_own,
    rstd_own,
    pg_ref,
    pg0,
    pg1,
    pg2,
    pg3,
    we_ref,
    wg_ref,
    wo_ref,
    gain_ref,
    ogain_ref,
    obias_ref,
    dz_ref,
    grads_ref,
    wgT,
    woT,
    vec,
    pm,
    pgs,
    pr,
    dgl_own,
    gacc,
):
    me = me_ref[0]
    rows, tokens, width = pg_ref.shape
    half = rows // 2
    hidden = wo_ref.shape[0]
    wgT[...] = transposed(wg_ref)
    woT[...] = transposed(wo_ref)
    vec[0] = columns_of(gain_ref)
    vec[1] = columns_of(ogain_ref)
    vec[2] = columns_of(obias_ref)
    fill_pair_mask(mask_ref, pm, rows)
    gacc[...] = jnp.zeros_like(gacc)
    for s, ref in enumerate((pg0, pg1, pg2, pg3)):
        at = pl.multiple_of(jnp.bitwise_xor(me, s) * rows * rows, rows * rows)
        pgs[pl.ds(at, rows * rows), :] = ref[...].reshape(rows * rows, width).astype(F32)

    @pl.loop(0, half, unroll=8)
    def _(t):
        for which in range(2):
            x = prod[which, pl.ds(t, hidden, stride=half), :].astype(BF16).astype(F32)
            xhat, rstd = norm_columns(x)
            if which == 0:
                zn = zn_own[t]
                pg = two_rows(pg_ref, t)
            else:
                zn = zn_cols[t]
                pg = jnp.concatenate(
                    [
                        pgs[pl.ds(t, tokens, stride=rows), :],
                        pgs[pl.ds(t + half, tokens, stride=rows), :],
                    ],
                    axis=0,
                ).T
            gate = jax.nn.sigmoid(dot(wgT[...], zn))
            dy = (pg * gate).astype(BF16)
            dxn = dot(wo_ref[...], dy)
            if which == 0:
                xn = (xhat * vec[1] + vec[2]).astype(BF16)
                y = dot(woT[...], xn)
                dgl = (pg * y * gate * (1.0 - gate)).astype(BF16)
                dgl_own[t] = dgl
                gacc[4] += dot_nt(zn, dgl)
                gacc[5] += dot_nt(xn, dy)
                gacc[6] += dxn * xhat
                gacc[7] += dxn
            pr[which, pl.ds(t, hidden, stride=half), :] = norm_columns_backward(
                dxn, vec[1], xhat, rstd
            )

    @pl.loop(0, hidden, unroll=32)
    def _(h):
        at = pl.ds(pl.multiple_of(h * half, half), half)
        pr[0, at, :] = lanes(dot(halves(pr[0, at, :]), right_sq[h]))
        pr[1, at, :] = lanes(dot(halves(pr[1, at, :]), left_sq[h]))

    @pl.loop(0, half, unroll=8)
    def _(t):
        mask = pm[pl.ds(me * half + t, 1), :]
        zn = zn_own[t]
        zhat = zhat_own[t]
        dzn = dot(wg_ref[...], dgl_own[t])
        for which in range(2):
            d = pr[which, pl.ds(t, hidden, stride=half), :].astype(BF16).astype(F32) * mask
            sig = jax.nn.sigmoid(pre_own[t, pl.ds(2 * which * hidden, hidden), :])
            val = pre_own[t, pl.ds((2 * which + 1) * hidden, hidden), :]
            dval = d * sig
            dgate = (dval * val * (1.0 - sig)).astype(BF16)
            dval = dval.astype(BF16)
            gacc[2 * which] += dot_nt(zn, dgate)
            gacc[2 * which + 1] += dot_nt(zn, dval)
            dzn += dot(we_ref[:, 2 * which * hidden : (2 * which + 1) * hidden], dgate)
            dzn += dot(we_ref[:, (2 * which + 1) * hidden : (2 * which + 2) * hidden], dval)
        gacc[8] += dzn * zhat
        gacc[9] += dzn
        dz = norm_columns_backward(dzn, vec[0], zhat, rstd_own[t]).T.astype(BF16)
        dz_ref[t] = dz[:tokens]
        dz_ref[t + half] = dz[tokens:]

    for b in range(6):
        grads_ref[b * LANES : (b + 1) * LANES, :] = gacc[b].astype(BF16)
    sums = [jnp.sum(gacc[b].T, axis=0, keepdims=True) for b in (8, 9, 6, 7)]
    pad = grads_ref.shape[0] - 6 * LANES
    sums.append(jnp.zeros((pad - 4, LANES), F32))
    grads_ref[6 * LANES :, :] = jnp.concatenate(sums, axis=0).astype(BF16)


def finish_kernel(n_blocks, me_ref, *refs):
    chunks = refs[:n_blocks]
    edges_ref, gate_ref, out_ref, in_norm_ref, out_norm_ref, total = refs[n_blocks:]
    me = me_ref[0]
    rows = chunks[0].shape[0]
    for s in range(n_blocks):
        at = pl.multiple_of(jnp.bitwise_xor(me, s) * rows, rows)
        total[pl.ds(at, rows), :] = chunks[s][...].astype(F32)
    for b in range(4):
        edges_ref[:, b * LANES : (b + 1) * LANES] = total[b * LANES : (b + 1) * LANES, :]
    gate_ref[...] = total[4 * LANES : 5 * LANES, :]
    out_ref[...] = total[5 * LANES : 6 * LANES, :]
    in_norm_ref[...] = total[6 * LANES : 6 * LANES + 2, :]
    out_norm_ref[...] = total[6 * LANES + 2 : 6 * LANES + 4, :]


def pick(x, i):
    return lax.dynamic_index_in_dim(x, i, 0, keepdims=False)


def swap(x, axis, n, bit):
    return lax.ppermute(x, axis, [(i, i ^ bit) for i in range(n)])


def bits_of(n):
    out = []
    b = n // 2
    while b:
        out.append(b)
        b //= 2
    return out


def per_device_fused(
    n_dp,
    n_dap,
    pair,
    pair_grad,
    token_mask,
    w_edges,
    w_gate,
    w_out,
    in_gain,
    in_bias,
    output_norm_gain,
    output_norm_bias,
):
    rows, tokens, width = pair.shape[1:]
    hidden = w_out.shape[0]
    me = lax.axis_index("dap")
    place = me.astype(jnp.int32).reshape(1)
    x = pair[0]
    g = pair_grad[0]

    half = rows // 2
    grad_rows = 6 * LANES + 16 * n_dap
    vm = pltpu.VMEM
    out = jax.ShapeDtypeStruct
    row = lambda v: v.reshape(1, -1)

    def call(kernel, us, outs, scratch, *args, in_hbm=0):
        whole = pl.BlockSpec(memory_space=pltpu.VMEM)
        hbm = pl.BlockSpec(memory_space=pltpu.HBM)
        return pl.pallas_call(
            kernel,
            out_shape=tuple(outs),
            in_specs=[pl.BlockSpec(memory_space=pltpu.SMEM)]
            + [whole] * (len(args) - in_hbm)
            + [hbm] * in_hbm,
            out_specs=(whole,) * len(outs),
            scratch_shapes=scratch,
            compiler_params=pltpu.CompilerParams(vmem_limit_bytes=VMEM_BYTES),
            cost_estimate=pl.CostEstimate(
                flops=0, bytes_accessed=int(us * 3.6e6), transcendentals=0
            ),
        )(place, *args)

    cut = g.reshape(rows, n_dap, rows, width)
    far = swap(x, "dap", n_dap, 2)
    near = swap(x, "dap", n_dap, 1)
    pg_own, *pgs = [lax.dynamic_index_in_dim(cut, me ^ s, 1, keepdims=False) for s in range(4)]
    pgs = [swap(v, "dap", n_dap, s) for s, v in enumerate(pgs, 1)]
    weT, ls, rs, pre_own, zn_own, zhat_own, rstd_own = call(
        near_kernel,
        4,
        [
            out((4 * hidden, width), BF16),
            out((2, hidden * half, LANES), F32),
            out((2, hidden * half, LANES), F32),
            out((half, 4 * hidden, LANES), F32),
            out((half, width, LANES), BF16),
            out((half, width, LANES), F32),
            out((half, 1, LANES), F32),
        ],
        [
            vm((2, width, LANES), F32),
            vm((n_dap * half, LANES), F32),
            vm((1, tokens), jnp.int32),
            vm((rows, tokens, width), BF16),
            vm((width, 4 * hidden), BF16),
            vm((1, width), F32),
            vm((1, width), F32),
            pltpu.SemaphoreType.DMA((5,)),
        ],
        near,
        token_mask,
        x,
        w_edges,
        row(in_gain),
        row(in_bias),
        in_hbm=5,
    )
    far, zn_own, pg_own = lax.optimization_barrier((far, zn_own, pg_own))
    across = swap(far, "dap", n_dap, 1)
    prod, left_sq, right_sq, zn_cols = call(
        product_kernel,
        8,
        [
            out((2, hidden * half, LANES), F32),
            out((hidden, tokens, tokens), BF16),
            out((hidden, tokens, tokens), BF16),
            out((half, width, LANES), BF16),
        ],
        [
            vm((2, width, LANES), F32),
            vm((n_dap * half, LANES), F32),
            vm((n_dap * rows * tokens, width), F32),
            vm((2, hidden * half, LANES), F32),
            vm((2, hidden * half, LANES), F32),
        ],
        token_mask,
        x,
        near,
        far,
        across,
        weT,
        ls,
        rs,
        row(in_gain),
        row(in_bias),
    )
    dz, grads = call(
        back_kernel,
        8,
        [out((rows, tokens, width), BF16), out((grad_rows, LANES), BF16)],
        [
            vm((width, width), BF16),
            vm((width, hidden), BF16),
            vm((3, width, LANES), F32),
            vm((n_dap * half, LANES), F32),
            vm((n_dap * rows * rows, width), F32),
            vm((2, hidden * half, LANES), F32),
            vm((half, width, LANES), BF16),
            vm((10, LANES, LANES), F32),
        ],
        token_mask,
        prod,
        left_sq,
        right_sq,
        zn_cols,
        pre_own,
        zn_own,
        zhat_own,
        rstd_own,
        g,
        pg_own,
        *pgs,
        w_edges,
        w_gate,
        w_out,
        row(in_gain),
        row(output_norm_gain),
        row(output_norm_bias),
    )

    chunks = grads.reshape(n_dap, -1, LANES)
    total = pick(chunks, me).astype(F32)
    got = [swap(pick(chunks, me ^ s), "dap", n_dap, s) for s in range(1, n_dap)]
    for c in got:
        total = total + c.astype(F32)
    total = total.astype(BF16)
    bits = bits_of(n_dp)[::-1]
    for i in range(0, len(bits), 2):
        terms = [total.astype(F32)]
        shifts = [0]
        for bit in bits[i : i + 2]:
            shifts += [s ^ bit for s in shifts]
        terms += [swap(total, "dp", n_dp, s).astype(F32) for s in shifts[1:]]
        while len(terms) > 1:
            terms = [p + q for p, q in zip(terms[::2], terms[1::2])]
        total = terms[0].astype(BF16)
    parts = [total] + [swap(total, "dap", n_dap, s) for s in range(1, n_dap)]
    edges, gate, outs, in_norm, out_norm = call(
        functools.partial(finish_kernel, n_dap),
        1,
        [
            out((width, 4 * hidden), F32),
            out((width, width), F32),
            out((hidden, width), F32),
            out((2, width), F32),
            out((2, hidden), F32),
        ],
        [vm((grad_rows, LANES), F32)],
        *parts,
    )
    return (dz[None], edges, gate, outs, in_norm, out_norm)


def solution(mesh):
    in_specs = (
        P("dp", "dap", None, None),
        P("dp", "dap", None, None),
        P("dp", None),
        P(),
        P(),
        P(),
        P(),
        P(),
        P(),
        P(),
    )
    out_specs = (P("dp", "dap", None, None), P(), P(), P(), P(), P())
    n_dp, n_dap = mesh.shape["dp"], mesh.shape["dap"]

    def per_device(pair, *others):
        structs, rows, tokens, width = pair.shape
        hidden = others[4].shape[0]
        fits = (
            structs == 1
            and 2 * tokens == LANES
            and rows == 16
            and width == LANES
            and hidden == LANES
            and n_dap == 4
            and n_dp & (n_dp - 1) == 0
        )
        if fits:
            return per_device_fused(n_dp, n_dap, pair, *others)
        return per_device_exchange(pair, *others)

    return jax.shard_map(
        per_device, mesh=mesh, in_specs=in_specs, out_specs=out_specs, check_vma=False
    )
```

```python
import functools

import jax
import jax.numpy as jnp
from jax import lax
from jax.experimental import pallas as pl
from jax.experimental.pallas import tpu as pltpu
from jax.sharding import PartitionSpec as P

EPS = 1e-05
LANES = 128
VMEM_BYTES = 32 * 1024 * 1024
F32 = jnp.float32
BF16 = jnp.bfloat16


def apply_layer_norm(values, reduce_dimension):
    mean = jnp.mean(values, axis=reduce_dimension, keepdims=True)
    var = jnp.mean((values - mean) ** 2, axis=reduce_dimension, keepdims=True)
    rstd = lax.rsqrt(var + EPS)
    return ((values - mean) * rstd, rstd)


def layer_norm_backward(dnorm, gain, normed, rstd, reduce_dimension):
    scaled = dnorm * gain
    return (
        scaled
        - jnp.mean(scaled, axis=reduce_dimension, keepdims=True)
        - normed * jnp.mean(scaled * normed, axis=reduce_dimension, keepdims=True)
    ) * rstd


def per_device_exchange(
    pair,
    pair_grad,
    token_mask,
    w_edges,
    w_gate,
    w_out,
    in_gain,
    in_bias,
    output_norm_gain,
    output_norm_bias,
):
    z_rows = pair[0]
    dout = pair_grad[0]
    rows = z_rows.shape[0]
    hidden = w_out.shape[0]
    width = w_gate.shape[0]
    first = lax.axis_index("dap") * rows
    mask_full = token_mask[0].astype(jnp.float32)
    mask_rows = lax.dynamic_slice_in_dim(mask_full, first, rows, 0)
    edge_mask = mask_rows[:, None, None] * mask_full[None, None, :]
    zhat, rstd_in = apply_layer_norm(z_rows.astype(jnp.float32), 2)
    zn = (zhat * in_gain + in_bias).astype(jnp.bfloat16)

    def project(columns):
        return jnp.einsum("ikc,ch->ihk", zn, columns, preferred_element_type=jnp.float32)

    def edge_values(pre):
        return (edge_mask * jax.nn.sigmoid(pre[:, :hidden]) * pre[:, hidden:]).astype(jnp.bfloat16)

    pre_left = project(w_edges[:, : 2 * hidden])
    pre_right = project(w_edges[:, 2 * hidden :])
    left_ch, right_ch = (
        lax.all_to_all(edge_values(pre_left), "dap", split_axis=1, concat_axis=0, tiled=True),
        lax.all_to_all(edge_values(pre_right), "dap", split_axis=1, concat_axis=0, tiled=True),
    )
    tri = jnp.einsum("ihk,jhk->ihj", left_ch, right_ch, preferred_element_type=jnp.float32).astype(
        jnp.bfloat16
    )
    triangle_product = lax.all_to_all(tri, "dap", split_axis=0, concat_axis=1, tiled=True)
    centered_scaled_input, output_inverse_deviation = apply_layer_norm(
        triangle_product.astype(jnp.float32), 1
    )
    normalized_product = (
        centered_scaled_input * output_norm_gain[None, :, None] + output_norm_bias[None, :, None]
    ).astype(jnp.bfloat16)
    gate = jax.nn.sigmoid(jnp.einsum("ijc,cd->ijd", zn, w_gate, preferred_element_type=jnp.float32))
    y_out = jnp.einsum("ihj,hc->ijc", normalized_product, w_out, preferred_element_type=jnp.float32)
    doutf = dout.astype(jnp.float32)
    dy = (doutf * gate).astype(jnp.bfloat16)
    dgl = (doutf * y_out * gate * (1.0 - gate)).astype(jnp.bfloat16)
    grad_out = jnp.einsum("ihj,ijc->hc", normalized_product, dy, preferred_element_type=jnp.float32)
    normalized_gradient = jnp.einsum("ijc,hc->ihj", dy, w_out, preferred_element_type=jnp.float32)
    output_norm_backward = jnp.stack(
        [
            jnp.sum(normalized_gradient * centered_scaled_input, axis=(0, 2)),
            jnp.sum(normalized_gradient, axis=(0, 2)),
        ]
    )
    product_gradient = layer_norm_backward(
        normalized_gradient,
        output_norm_gain[None, :, None],
        centered_scaled_input,
        output_inverse_deviation,
        1,
    ).astype(jnp.bfloat16)
    dprod_ch = lax.all_to_all(product_gradient, "dap", split_axis=1, concat_axis=0, tiled=True)
    dleft_ch = jnp.einsum(
        "ihj,jhk->ihk", dprod_ch, right_ch, preferred_element_type=jnp.float32
    ).astype(jnp.bfloat16)
    dright_ch = jnp.einsum(
        "ihj,ihk->jhk", dprod_ch, left_ch, preferred_element_type=jnp.float32
    ).astype(jnp.bfloat16)
    dleft, dright = (
        lax.all_to_all(dleft_ch, "dap", split_axis=0, concat_axis=1, tiled=True),
        lax.all_to_all(dright_ch, "dap", split_axis=0, concat_axis=1, tiled=True),
    )

    def pre_grad(dvalues, pre):
        sig = jax.nn.sigmoid(pre[:, :hidden])
        masked = dvalues.astype(jnp.float32) * edge_mask
        return jnp.concatenate(
            [masked * pre[:, hidden:] * sig * (1.0 - sig), masked * sig], axis=1
        ).astype(jnp.bfloat16)

    dpre_left = pre_grad(dleft, pre_left)
    dpre_right = pre_grad(dright, pre_right)
    grad_edges = jnp.concatenate(
        [
            jnp.einsum("ikc,ihk->ch", zn, dpre_left, preferred_element_type=jnp.float32),
            jnp.einsum("ikc,ihk->ch", zn, dpre_right, preferred_element_type=jnp.float32),
        ],
        axis=1,
    )
    grad_gate = jnp.einsum("ijc,ijd->cd", zn, dgl, preferred_element_type=jnp.float32)
    dzn = jnp.einsum(
        "ihk,ch->ikc", dpre_left, w_edges[:, : 2 * hidden], preferred_element_type=jnp.float32
    )
    dzn = dzn + jnp.einsum(
        "ihk,ch->ikc", dpre_right, w_edges[:, 2 * hidden :], preferred_element_type=jnp.float32
    )
    dzn = dzn + jnp.einsum("ijd,cd->ijc", dgl, w_gate, preferred_element_type=jnp.float32)
    in_norm_grad = jnp.stack([jnp.sum(dzn * zhat, axis=(0, 1)), jnp.sum(dzn, axis=(0, 1))])
    dz = layer_norm_backward(dzn, in_gain, zhat, rstd_in, 2).astype(jnp.bfloat16)
    flat = jnp.concatenate(
        [
            grad_edges.ravel(),
            grad_gate.ravel(),
            grad_out.ravel(),
            in_norm_grad.ravel(),
            output_norm_backward.ravel(),
        ]
    )
    summed = lax.psum(flat, ("dp", "dap"))
    edge_size = width * 4 * hidden
    gate_size = width * width
    out_size = hidden * width
    offset = 0
    total_edges = summed[offset : offset + edge_size].reshape(width, 4 * hidden)
    offset = offset + edge_size
    total_gate = summed[offset : offset + gate_size].reshape(width, width)
    offset = offset + gate_size
    total_out = summed[offset : offset + out_size].reshape(hidden, width)
    offset = offset + out_size
    total_in_norm = summed[offset : offset + 2 * width].reshape(2, width)
    offset = offset + 2 * width
    total_out_norm = summed[offset : offset + 2 * hidden].reshape(2, hidden)
    return (dz[None], total_edges, total_gate, total_out, total_in_norm, total_out_norm)


def dot(a, b):
    return jnp.dot(a, b, preferred_element_type=F32)


def dot_nt(a, b):
    return lax.dot_general(a, b, (((1,), (1,)), ((), ())), preferred_element_type=F32)


def norm_columns(x):
    mean = jnp.mean(x, axis=0, keepdims=True)
    centred = x - mean
    var = jnp.mean(centred * centred, axis=0, keepdims=True)
    rstd = lax.rsqrt(var + EPS)
    return centred * rstd, rstd


def norm_columns_backward(dnorm, gain, normed, rstd):
    scaled = dnorm * gain
    m1 = jnp.mean(scaled, axis=0, keepdims=True)
    m2 = jnp.mean(scaled * normed, axis=0, keepdims=True)
    return (scaled - m1 - normed * m2) * rstd


def halves(x):
    n = LANES // 2
    return jnp.concatenate([x[:, :n], x[:, n:]], axis=0).astype(BF16)


def lanes(x):
    return jnp.concatenate([x[:8], x[8:]], axis=1)


def square(blocks):
    n = LANES // 2
    return jnp.concatenate([p for x in blocks for p in (x[:, :n], x[:, n:])], axis=0).astype(BF16)


def columns_of(ref):
    return jnp.broadcast_to(ref[...], (ref.shape[1], LANES)).T


def transposed(ref):
    return ref[...].astype(F32).T.astype(BF16)


def fill_pair_mask(mask_ref, pm, rows):
    half = rows // 2
    low = lax.broadcasted_iota(jnp.int32, (half, LANES), 1) < LANES // 2
    m = mask_ref[...].astype(F32)
    m = jnp.broadcast_to(jnp.concatenate([m, m], axis=1), (LANES, LANES))
    mt = m.T
    for a in range(pm.shape[0] // half):
        lo = mt[rows * a : rows * a + half]
        hi = mt[rows * a + half : rows * (a + 1)]
        pm[half * a : half * (a + 1), :] = jnp.where(low, lo, hi) * m[:half]


def two_rows(ref, t):
    half = ref.shape[0] // 2
    return jnp.concatenate([ref[t].astype(F32), ref[t + half].astype(F32)], axis=0).T


def edge_tile(pair_ref, t, block, place, weT, vec, pm, ls, rs):
    half = pair_ref.shape[0] // 2
    hidden = weT.shape[0] // 4
    zhat, rstd = norm_columns(two_rows(pair_ref, t))
    zn = (zhat * vec[0] + vec[1]).astype(BF16)
    pre = dot(weT[...], zn)
    mask = pm[pl.ds(block * half + t, 1), :]
    ls[place, pl.ds(t, hidden, stride=half), :] = (
        mask * jax.nn.sigmoid(pre[:hidden]) * pre[hidden : 2 * hidden]
    )
    rs[place, pl.ds(t, hidden, stride=half), :] = (
        mask * jax.nn.sigmoid(pre[2 * hidden : 3 * hidden]) * pre[3 * hidden :]
    )
    return zhat, rstd, zn, pre


def near_kernel(
    me_ref,
    near_ref,
    mask_hbm,
    own_hbm,
    we_hbm,
    gain_hbm,
    bias_hbm,
    weT,
    ls,
    rs,
    factors,
    zn_own,
    zhat_own,
    rstd_own,
    vec,
    pm,
    near_x,
    mask_ref,
    own_ref,
    we_ref,
    gain_ref,
    bias_ref,
    sems,
):
    me = me_ref[0]
    copies = [
        pltpu.make_async_copy(src, dst, sems.at[i])
        for i, (src, dst) in enumerate(
            (
                (we_hbm, we_ref),
                (own_hbm, own_ref),
                (mask_hbm, mask_ref),
                (gain_hbm, gain_ref),
                (bias_hbm, bias_ref),
            )
        )
    ]
    for copy in copies:
        copy.start()
    for copy in copies:
        copy.wait()
    rows = own_ref.shape[0]
    half = rows // 2
    hidden = we_ref.shape[1] // 4
    for b in range(4):
        cols = slice(b * hidden, (b + 1) * hidden)
        weT[cols, :] = we_ref[:, cols].astype(F32).T.astype(BF16)
    vec[0] = columns_of(gain_ref)
    vec[1] = columns_of(bias_ref)
    fill_pair_mask(mask_ref, pm, rows)
    for s, ref in enumerate((own_ref, near_ref)):
        block = jnp.bitwise_xor(me, s)
        place = jnp.bitwise_and(block, 1)
        near_x[place] = ref[...].astype(F32).reshape(near_x.shape[1:])

        @pl.loop(0, half, unroll=8)
        def _(t, s=s, ref=ref, block=block, place=place):
            zhat, rstd, zn, pre = edge_tile(ref, t, block, place, weT, vec, pm, ls, rs)
            if s == 0:
                mask = pm[pl.ds(block * half + t, 1), :]
                for which in range(2):
                    at = 2 * which * hidden
                    sig = jax.nn.sigmoid(pre[at : at + hidden])
                    val = pre[at + hidden : at + 2 * hidden]
                    masked = mask * sig
                    factors[t, at : at + hidden, :] = masked * val * (1.0 - sig)
                    factors[t, at + hidden : at + 2 * hidden, :] = masked
                zn_own[t] = zn
                zhat_own[t] = zhat
                rstd_own[t] = rstd


def product_kernel(
    me_ref,
    pair2,
    pair3,
    weT,
    near_ls,
    near_rs,
    vec,
    pm,
    near_x,
    prod,
    left_sq,
    right_sq,
    zn_cols,
    far_x,
    far_ls,
    far_rs,
):
    me = me_ref[0]
    rows, tokens, _ = pair2.shape
    half = rows // 2
    hidden = weT.shape[0] // 4
    for s, ref in ((2, pair2), (3, pair3)):
        block = jnp.bitwise_xor(me, s)
        place = jnp.bitwise_and(block, 1)

        @pl.loop(0, half, unroll=8)
        def _(t, ref=ref, block=block, place=place):
            edge_tile(ref, t, block, place, weT, vec, pm, far_ls, far_rs)

        far_x[place] = ref[...].astype(F32).reshape(far_x.shape[1:])

    core = jnp.bitwise_and(me, 1)
    group = me // 2
    n_near = pl.multiple_of(group * 2 * rows, 2 * rows)
    n_far = pl.multiple_of((1 - group) * 2 * rows, 2 * rows)

    @pl.loop(0, hidden, unroll=32)
    def _(h):
        at = pl.ds(pl.multiple_of(h * half, half), half)
        for near, far, sq in ((near_ls, far_ls, left_sq), (near_rs, far_rs, right_sq)):
            sq[h, pl.ds(n_near, 2 * rows), :] = square((near[0, at, :], near[1, at, :]))
            sq[h, pl.ds(n_far, 2 * rows), :] = square((far[0, at, :], far[1, at, :]))
        prod[0, at, :] = lanes(dot_nt(halves(near_ls[core, at, :]), right_sq[h]))
        prod[1, at, :] = lanes(dot_nt(halves(near_rs[core, at, :]), left_sq[h]))

    @pl.loop(0, half, unroll=8)
    def _(t):
        x = []
        for j in (me * rows + t, me * rows + t + half):
            near, far = (
                jnp.concatenate(
                    [v[p, pl.ds(j, rows, stride=tokens), :] for p in range(2)], axis=0
                )
                for v in (near_x, far_x)
            )
            x += [jnp.where(group == 0, near, far), jnp.where(group == 0, far, near)]
        x = jnp.concatenate(x, axis=0).T
        zhat, _ = norm_columns(x)
        zn_cols[t] = (zhat * vec[0] + vec[1]).astype(BF16)


def back_kernel(
    me_ref,
    prod,
    left_sq,
    right_sq,
    zn_cols,
    factors,
    zn_own,
    zhat_own,
    pg_ref,
    pg0,
    pg1,
    pg2,
    pg3,
    we_ref,
    wg_ref,
    wo_ref,
    ogain_ref,
    obias_ref,
    dzn_ref,
    grads_ref,
    wgT,
    woT,
    vec,
    pgs,
    pr,
    dgl_own,
    gacc,
):
    me = me_ref[0]
    rows, tokens, width = pg_ref.shape
    half = rows // 2
    hidden = wo_ref.shape[0]
    wgT[...] = transposed(wg_ref)
    woT[...] = transposed(wo_ref)
    vec[0] = columns_of(ogain_ref)
    vec[1] = columns_of(obias_ref)
    gacc[...] = jnp.zeros_like(gacc)
    for s, ref in enumerate((pg0, pg1, pg2, pg3)):
        at = pl.multiple_of(jnp.bitwise_xor(me, s) * rows * rows, rows * rows)
        pgs[pl.ds(at, rows * rows), :] = ref[...].reshape(rows * rows, width).astype(F32)

    @pl.loop(0, half, unroll=8)
    def _(t):
        for which in range(2):
            x = prod[which, pl.ds(t, hidden, stride=half), :].astype(BF16).astype(F32)
            xhat, rstd = norm_columns(x)
            if which == 0:
                zn = zn_own[t]
                pg = two_rows(pg_ref, t)
            else:
                zn = zn_cols[t]
                pg = jnp.concatenate(
                    [
                        pgs[pl.ds(t, tokens, stride=rows), :],
                        pgs[pl.ds(t + half, tokens, stride=rows), :],
                    ],
                    axis=0,
                ).T
            gate = jax.nn.sigmoid(dot(wgT[...], zn))
            dy = (pg * gate).astype(BF16)
            dxn = dot(wo_ref[...], dy)
            if which == 0:
                xn = (xhat * vec[0] + vec[1]).astype(BF16)
                y = dot(woT[...], xn)
                dgl = (pg * y * gate * (1.0 - gate)).astype(BF16)
                dgl_own[t] = dgl
                gacc[4] += dot_nt(zn, dgl)
                gacc[5] += dot_nt(xn, dy)
                gacc[6] += dxn * xhat
                gacc[7] += dxn
            pr[which, pl.ds(t, hidden, stride=half), :] = norm_columns_backward(
                dxn, vec[0], xhat, rstd
            )

    @pl.loop(0, hidden, unroll=32)
    def _(h):
        at = pl.ds(pl.multiple_of(h * half, half), half)
        pr[0, at, :] = lanes(dot(halves(pr[0, at, :]), right_sq[h]))
        pr[1, at, :] = lanes(dot(halves(pr[1, at, :]), left_sq[h]))

    @pl.loop(0, half, unroll=8)
    def _(t):
        zn = zn_own[t]
        zhat = zhat_own[t]
        dzn = dot(wg_ref[...], dgl_own[t])
        for which in range(2):
            d = pr[which, pl.ds(t, hidden, stride=half), :].astype(BF16).astype(F32)
            for b in (2 * which, 2 * which + 1):
                cols = slice(b * hidden, (b + 1) * hidden)
                dpre = (d * factors[t, cols, :]).astype(BF16)
                gacc[b] += dot_nt(zn, dpre)
                dzn += dot(we_ref[:, cols], dpre)
        gacc[8] += dzn * zhat
        gacc[9] += dzn
        dzn_ref[t] = dzn

    for b in range(6):
        grads_ref[b * LANES : (b + 1) * LANES, :] = gacc[b].astype(BF16)
    sums = [jnp.sum(gacc[b].T, axis=0, keepdims=True) for b in (8, 9, 6, 7)]
    pad = grads_ref.shape[0] - 6 * LANES
    sums.append(jnp.zeros((pad - 4, LANES), F32))
    grads_ref[6 * LANES :, :] = jnp.concatenate(sums, axis=0).astype(BF16)


def input_kernel(me_ref, dzn_ref, zhat_own, rstd_own, vec, dz_ref):
    half = dzn_ref.shape[0]
    tokens = dz_ref.shape[1]
    gain = vec[0]
    for t in range(half):
        dz = norm_columns_backward(dzn_ref[t], gain, zhat_own[t], rstd_own[t]).T.astype(BF16)
        dz_ref[t] = dz[:tokens]
        dz_ref[t + half] = dz[tokens:]


def finish_kernel(n_blocks, me_ref, *refs):
    chunks = refs[:n_blocks]
    edges_ref, gate_ref, out_ref, in_norm_ref, out_norm_ref, total = refs[n_blocks:]
    me = me_ref[0]
    rows = chunks[0].shape[0]
    for s in range(n_blocks):
        at = pl.multiple_of(jnp.bitwise_xor(me, s) * rows, rows)
        total[pl.ds(at, rows), :] = chunks[s][...].astype(F32)
    for b in range(4):
        edges_ref[:, b * LANES : (b + 1) * LANES] = total[b * LANES : (b + 1) * LANES, :]
    gate_ref[...] = total[4 * LANES : 5 * LANES, :]
    out_ref[...] = total[5 * LANES : 6 * LANES, :]
    in_norm_ref[...] = total[6 * LANES : 6 * LANES + 2, :]
    out_norm_ref[...] = total[6 * LANES + 2 : 6 * LANES + 4, :]


def pick(x, i):
    return lax.dynamic_index_in_dim(x, i, 0, keepdims=False)


def swap(x, axis, n, bit):
    return lax.ppermute(x, axis, [(i, i ^ bit) for i in range(n)])


def bits_of(n):
    out = []
    b = n // 2
    while b:
        out.append(b)
        b //= 2
    return out


def per_device_fused(
    n_dp,
    n_dap,
    pair,
    pair_grad,
    token_mask,
    w_edges,
    w_gate,
    w_out,
    in_gain,
    in_bias,
    output_norm_gain,
    output_norm_bias,
):
    rows, tokens, width = pair.shape[1:]
    hidden = w_out.shape[0]
    me = lax.axis_index("dap")
    place = me.astype(jnp.int32).reshape(1)
    x = pair[0]
    g = pair_grad[0]

    half = rows // 2
    grad_rows = 6 * LANES + 16 * n_dap
    vm = pltpu.VMEM
    out = jax.ShapeDtypeStruct
    row = lambda v: v.reshape(1, -1)

    def call(kernel, us, outs, scratch, *args, in_hbm=0):
        whole = pl.BlockSpec(memory_space=pltpu.VMEM)
        hbm = pl.BlockSpec(memory_space=pltpu.HBM)
        return pl.pallas_call(
            kernel,
            out_shape=tuple(outs),
            in_specs=[pl.BlockSpec(memory_space=pltpu.SMEM)]
            + [whole] * (len(args) - in_hbm)
            + [hbm] * in_hbm,
            out_specs=(whole,) * len(outs),
            scratch_shapes=scratch,
            compiler_params=pltpu.CompilerParams(vmem_limit_bytes=VMEM_BYTES),
            cost_estimate=pl.CostEstimate(
                flops=0, bytes_accessed=int(us * 3.6e6), transcendentals=0
            ),
        )(place, *args)

    cut = g.reshape(rows, n_dap, rows, width)
    far = swap(x, "dap", n_dap, 2)
    near = swap(x, "dap", n_dap, 1)
    pg_own, *pgs = [lax.dynamic_index_in_dim(cut, me ^ s, 1, keepdims=False) for s in range(4)]
    pgs = [swap(v, "dap", n_dap, s) for s, v in enumerate(pgs, 1)]
    weT, ls, rs, factors, zn_own, zhat_own, rstd_own, vec, pm, near_x = call(
        near_kernel,
        4,
        [
            out((4 * hidden, width), BF16),
            out((2, hidden * half, LANES), F32),
            out((2, hidden * half, LANES), F32),
            out((half, 4 * hidden, LANES), F32),
            out((half, width, LANES), BF16),
            out((half, width, LANES), F32),
            out((half, 1, LANES), F32),
            out((2, width, LANES), F32),
            out((n_dap * half, LANES), F32),
            out((2, rows * tokens, width), F32),
        ],
        [
            vm((1, tokens), jnp.int32),
            vm((rows, tokens, width), BF16),
            vm((width, 4 * hidden), BF16),
            vm((1, width), F32),
            vm((1, width), F32),
            pltpu.SemaphoreType.DMA((5,)),
        ],
        near,
        token_mask,
        x,
        w_edges,
        row(in_gain),
        row(in_bias),
        in_hbm=5,
    )
    far, zn_own, pg_own = lax.optimization_barrier((far, zn_own, pg_own))
    across = swap(far, "dap", n_dap, 1)
    prod, left_sq, right_sq, zn_cols = call(
        product_kernel,
        8,
        [
            out((2, hidden * half, LANES), F32),
            out((hidden, tokens, tokens), BF16),
            out((hidden, tokens, tokens), BF16),
            out((half, width, LANES), BF16),
        ],
        [
            vm((2, rows * tokens, width), F32),
            vm((2, hidden * half, LANES), F32),
            vm((2, hidden * half, LANES), F32),
        ],
        far,
        across,
        weT,
        ls,
        rs,
        vec,
        pm,
        near_x,
    )
    dzn, grads = call(
        back_kernel,
        8,
        [out((half, width, LANES), F32), out((grad_rows, LANES), BF16)],
        [
            vm((width, width), BF16),
            vm((width, hidden), BF16),
            vm((2, width, LANES), F32),
            vm((n_dap * rows * rows, width), F32),
            vm((2, hidden * half, LANES), F32),
            vm((half, width, LANES), BF16),
            vm((10, LANES, LANES), F32),
        ],
        prod,
        left_sq,
        right_sq,
        zn_cols,
        factors,
        zn_own,
        zhat_own,
        g,
        pg_own,
        *pgs,
        w_edges,
        w_gate,
        w_out,
        row(output_norm_gain),
        row(output_norm_bias),
    )
    (dz,) = call(
        input_kernel,
        1,
        [out((rows, tokens, width), BF16)],
        [],
        dzn,
        zhat_own,
        rstd_own,
        vec,
    )

    chunks = grads.reshape(n_dap, -1, LANES)
    total = pick(chunks, me).astype(F32)
    got = [swap(pick(chunks, me ^ s), "dap", n_dap, s) for s in range(1, n_dap)]
    for c in got:
        total = total + c.astype(F32)
    total = total.astype(BF16)
    bits = bits_of(n_dp)[::-1]
    for i in range(0, len(bits), 2):
        terms = [total.astype(F32)]
        shifts = [0]
        for bit in bits[i : i + 2]:
            shifts += [s ^ bit for s in shifts]
        terms += [swap(total, "dp", n_dp, s).astype(F32) for s in shifts[1:]]
        while len(terms) > 1:
            terms = [p + q for p, q in zip(terms[::2], terms[1::2])]
        total = terms[0].astype(BF16)
    parts = [total] + [swap(total, "dap", n_dap, s) for s in range(1, n_dap)]
    edges, gate, outs, in_norm, out_norm = call(
        functools.partial(finish_kernel, n_dap),
        1,
        [
            out((width, 4 * hidden), F32),
            out((width, width), F32),
            out((hidden, width), F32),
            out((2, width), F32),
            out((2, hidden), F32),
        ],
        [vm((grad_rows, LANES), F32)],
        *parts,
    )
    return (dz[None], edges, gate, outs, in_norm, out_norm)


def solution(mesh):
    in_specs = (
        P("dp", "dap", None, None),
        P("dp", "dap", None, None),
        P("dp", None),
        P(),
        P(),
        P(),
        P(),
        P(),
        P(),
        P(),
    )
    out_specs = (P("dp", "dap", None, None), P(), P(), P(), P(), P())
    n_dp, n_dap = mesh.shape["dp"], mesh.shape["dap"]

    def per_device(pair, *others):
        structs, rows, tokens, width = pair.shape
        hidden = others[4].shape[0]
        fits = (
            structs == 1
            and 2 * tokens == LANES
            and rows == 16
            and width == LANES
            and hidden == LANES
            and n_dap == 4
            and n_dp & (n_dp - 1) == 0
        )
        if fits:
            return per_device_fused(n_dp, n_dap, pair, *others)
        return per_device_exchange(pair, *others)

    return jax.shard_map(
        per_device, mesh=mesh, in_specs=in_specs, out_specs=out_specs, check_vma=False
    )
```

```python
import functools

import jax
import jax.numpy as jnp
from jax import lax
from jax.experimental import pallas as pl
from jax.experimental.pallas import tpu as pltpu
from jax.sharding import PartitionSpec as P

EPS = 1e-05
LANES = 128
VMEM_BYTES = 32 * 1024 * 1024
F32 = jnp.float32
BF16 = jnp.bfloat16


def apply_layer_norm(values, reduce_dimension):
    mean = jnp.mean(values, axis=reduce_dimension, keepdims=True)
    var = jnp.mean((values - mean) ** 2, axis=reduce_dimension, keepdims=True)
    rstd = lax.rsqrt(var + EPS)
    return ((values - mean) * rstd, rstd)


def layer_norm_backward(dnorm, gain, normed, rstd, reduce_dimension):
    scaled = dnorm * gain
    return (
        scaled
        - jnp.mean(scaled, axis=reduce_dimension, keepdims=True)
        - normed * jnp.mean(scaled * normed, axis=reduce_dimension, keepdims=True)
    ) * rstd


def per_device_exchange(
    pair,
    pair_grad,
    token_mask,
    w_edges,
    w_gate,
    w_out,
    in_gain,
    in_bias,
    output_norm_gain,
    output_norm_bias,
):
    z_rows = pair[0]
    dout = pair_grad[0]
    rows = z_rows.shape[0]
    hidden = w_out.shape[0]
    width = w_gate.shape[0]
    first = lax.axis_index("dap") * rows
    mask_full = token_mask[0].astype(jnp.float32)
    mask_rows = lax.dynamic_slice_in_dim(mask_full, first, rows, 0)
    edge_mask = mask_rows[:, None, None] * mask_full[None, None, :]
    zhat, rstd_in = apply_layer_norm(z_rows.astype(jnp.float32), 2)
    zn = (zhat * in_gain + in_bias).astype(jnp.bfloat16)

    def project(columns):
        return jnp.einsum("ikc,ch->ihk", zn, columns, preferred_element_type=jnp.float32)

    def edge_values(pre):
        return (edge_mask * jax.nn.sigmoid(pre[:, :hidden]) * pre[:, hidden:]).astype(jnp.bfloat16)

    pre_left = project(w_edges[:, : 2 * hidden])
    pre_right = project(w_edges[:, 2 * hidden :])
    left_ch, right_ch = (
        lax.all_to_all(edge_values(pre_left), "dap", split_axis=1, concat_axis=0, tiled=True),
        lax.all_to_all(edge_values(pre_right), "dap", split_axis=1, concat_axis=0, tiled=True),
    )
    tri = jnp.einsum("ihk,jhk->ihj", left_ch, right_ch, preferred_element_type=jnp.float32).astype(
        jnp.bfloat16
    )
    triangle_product = lax.all_to_all(tri, "dap", split_axis=0, concat_axis=1, tiled=True)
    centered_scaled_input, output_inverse_deviation = apply_layer_norm(
        triangle_product.astype(jnp.float32), 1
    )
    normalized_product = (
        centered_scaled_input * output_norm_gain[None, :, None] + output_norm_bias[None, :, None]
    ).astype(jnp.bfloat16)
    gate = jax.nn.sigmoid(jnp.einsum("ijc,cd->ijd", zn, w_gate, preferred_element_type=jnp.float32))
    y_out = jnp.einsum("ihj,hc->ijc", normalized_product, w_out, preferred_element_type=jnp.float32)
    doutf = dout.astype(jnp.float32)
    dy = (doutf * gate).astype(jnp.bfloat16)
    dgl = (doutf * y_out * gate * (1.0 - gate)).astype(jnp.bfloat16)
    grad_out = jnp.einsum("ihj,ijc->hc", normalized_product, dy, preferred_element_type=jnp.float32)
    normalized_gradient = jnp.einsum("ijc,hc->ihj", dy, w_out, preferred_element_type=jnp.float32)
    output_norm_backward = jnp.stack(
        [
            jnp.sum(normalized_gradient * centered_scaled_input, axis=(0, 2)),
            jnp.sum(normalized_gradient, axis=(0, 2)),
        ]
    )
    product_gradient = layer_norm_backward(
        normalized_gradient,
        output_norm_gain[None, :, None],
        centered_scaled_input,
        output_inverse_deviation,
        1,
    ).astype(jnp.bfloat16)
    dprod_ch = lax.all_to_all(product_gradient, "dap", split_axis=1, concat_axis=0, tiled=True)
    dleft_ch = jnp.einsum(
        "ihj,jhk->ihk", dprod_ch, right_ch, preferred_element_type=jnp.float32
    ).astype(jnp.bfloat16)
    dright_ch = jnp.einsum(
        "ihj,ihk->jhk", dprod_ch, left_ch, preferred_element_type=jnp.float32
    ).astype(jnp.bfloat16)
    dleft, dright = (
        lax.all_to_all(dleft_ch, "dap", split_axis=0, concat_axis=1, tiled=True),
        lax.all_to_all(dright_ch, "dap", split_axis=0, concat_axis=1, tiled=True),
    )

    def pre_grad(dvalues, pre):
        sig = jax.nn.sigmoid(pre[:, :hidden])
        masked = dvalues.astype(jnp.float32) * edge_mask
        return jnp.concatenate(
            [masked * pre[:, hidden:] * sig * (1.0 - sig), masked * sig], axis=1
        ).astype(jnp.bfloat16)

    dpre_left = pre_grad(dleft, pre_left)
    dpre_right = pre_grad(dright, pre_right)
    grad_edges = jnp.concatenate(
        [
            jnp.einsum("ikc,ihk->ch", zn, dpre_left, preferred_element_type=jnp.float32),
            jnp.einsum("ikc,ihk->ch", zn, dpre_right, preferred_element_type=jnp.float32),
        ],
        axis=1,
    )
    grad_gate = jnp.einsum("ijc,ijd->cd", zn, dgl, preferred_element_type=jnp.float32)
    dzn = jnp.einsum(
        "ihk,ch->ikc", dpre_left, w_edges[:, : 2 * hidden], preferred_element_type=jnp.float32
    )
    dzn = dzn + jnp.einsum(
        "ihk,ch->ikc", dpre_right, w_edges[:, 2 * hidden :], preferred_element_type=jnp.float32
    )
    dzn = dzn + jnp.einsum("ijd,cd->ijc", dgl, w_gate, preferred_element_type=jnp.float32)
    in_norm_grad = jnp.stack([jnp.sum(dzn * zhat, axis=(0, 1)), jnp.sum(dzn, axis=(0, 1))])
    dz = layer_norm_backward(dzn, in_gain, zhat, rstd_in, 2).astype(jnp.bfloat16)
    flat = jnp.concatenate(
        [
            grad_edges.ravel(),
            grad_gate.ravel(),
            grad_out.ravel(),
            in_norm_grad.ravel(),
            output_norm_backward.ravel(),
        ]
    )
    summed = lax.psum(flat, ("dp", "dap"))
    edge_size = width * 4 * hidden
    gate_size = width * width
    out_size = hidden * width
    offset = 0
    total_edges = summed[offset : offset + edge_size].reshape(width, 4 * hidden)
    offset = offset + edge_size
    total_gate = summed[offset : offset + gate_size].reshape(width, width)
    offset = offset + gate_size
    total_out = summed[offset : offset + out_size].reshape(hidden, width)
    offset = offset + out_size
    total_in_norm = summed[offset : offset + 2 * width].reshape(2, width)
    offset = offset + 2 * width
    total_out_norm = summed[offset : offset + 2 * hidden].reshape(2, hidden)
    return (dz[None], total_edges, total_gate, total_out, total_in_norm, total_out_norm)


def dot(a, b):
    return jnp.dot(a, b, preferred_element_type=F32)


def dot_nt(a, b):
    return lax.dot_general(a, b, (((1,), (1,)), ((), ())), preferred_element_type=F32)


def norm_columns(x):
    mean = jnp.mean(x, axis=0, keepdims=True)
    centred = x - mean
    var = jnp.mean(centred * centred, axis=0, keepdims=True)
    rstd = lax.rsqrt(var + EPS)
    return centred * rstd, rstd


def norm_columns_backward(dnorm, gain, normed, rstd):
    scaled = dnorm * gain
    m1 = jnp.mean(scaled, axis=0, keepdims=True)
    m2 = jnp.mean(scaled * normed, axis=0, keepdims=True)
    return (scaled - m1 - normed * m2) * rstd


def halves(x):
    n = LANES // 2
    return jnp.concatenate([x[:, :n], x[:, n:]], axis=0).astype(BF16)


def lanes(x):
    return jnp.concatenate([x[:8], x[8:]], axis=1)


def square(blocks):
    n = LANES // 2
    return jnp.concatenate([p for x in blocks for p in (x[:, :n], x[:, n:])], axis=0).astype(BF16)


def columns_of(ref):
    return jnp.broadcast_to(ref[...], (ref.shape[1], LANES)).T


def transposed(ref):
    return ref[...].astype(F32).T.astype(BF16)


def fill_pair_mask(mask_ref, pm, rows):
    half = rows // 2
    low = lax.broadcasted_iota(jnp.int32, (half, LANES), 1) < LANES // 2
    m = mask_ref[...].astype(F32)
    m = jnp.broadcast_to(jnp.concatenate([m, m], axis=1), (LANES, LANES))
    mt = m.T
    for a in range(pm.shape[0] // half):
        lo = mt[rows * a : rows * a + half]
        hi = mt[rows * a + half : rows * (a + 1)]
        pm[half * a : half * (a + 1), :] = jnp.where(low, lo, hi) * m[:half]


def two_rows(ref, t):
    half = ref.shape[0] // 2
    return jnp.concatenate([ref[t].astype(F32), ref[t + half].astype(F32)], axis=0).T


def edge_tile(pair_ref, t, block, place, weT, vec, pm, ls, rs):
    half = pair_ref.shape[0] // 2
    hidden = weT.shape[0] // 4
    zhat, rstd = norm_columns(two_rows(pair_ref, t))
    zn = (zhat * vec[0] + vec[1]).astype(BF16)
    pre = dot(weT[...], zn)
    mask = pm[pl.ds(block * half + t, 1), :]
    ls[place, pl.ds(t, hidden, stride=half), :] = (
        mask * jax.nn.sigmoid(pre[:hidden]) * pre[hidden : 2 * hidden]
    )
    rs[place, pl.ds(t, hidden, stride=half), :] = (
        mask * jax.nn.sigmoid(pre[2 * hidden : 3 * hidden]) * pre[3 * hidden :]
    )
    return zhat, rstd, zn, pre


def near_kernel(
    me_ref,
    near_ref,
    mask_hbm,
    own_hbm,
    we_hbm,
    gain_hbm,
    bias_hbm,
    weT,
    ls,
    rs,
    factors,
    zn_own,
    zhat_own,
    rstd_own,
    vec,
    pm,
    near_x,
    mask_ref,
    own_ref,
    we_ref,
    gain_ref,
    bias_ref,
    sems,
):
    me = me_ref[0]
    copies = [
        pltpu.make_async_copy(src, dst, sems.at[i])
        for i, (src, dst) in enumerate(
            (
                (we_hbm, we_ref),
                (own_hbm, own_ref),
                (mask_hbm, mask_ref),
                (gain_hbm, gain_ref),
                (bias_hbm, bias_ref),
            )
        )
    ]
    for copy in copies:
        copy.start()
    for copy in copies:
        copy.wait()
    rows = own_ref.shape[0]
    half = rows // 2
    hidden = we_ref.shape[1] // 4
    for b in range(4):
        cols = slice(b * hidden, (b + 1) * hidden)
        weT[cols, :] = we_ref[:, cols].astype(F32).T.astype(BF16)
    vec[0] = columns_of(gain_ref)
    vec[1] = columns_of(bias_ref)
    fill_pair_mask(mask_ref, pm, rows)
    for s, ref in enumerate((own_ref, near_ref)):
        block = jnp.bitwise_xor(me, s)
        place = jnp.bitwise_and(block, 1)
        near_x[place] = ref[...].astype(F32).reshape(near_x.shape[1:])

        @pl.loop(0, half, unroll=8)
        def _(t, s=s, ref=ref, block=block, place=place):
            zhat, rstd, zn, pre = edge_tile(ref, t, block, place, weT, vec, pm, ls, rs)
            if s == 0:
                mask = pm[pl.ds(block * half + t, 1), :]
                for which in range(2):
                    at = 2 * which * hidden
                    sig = jax.nn.sigmoid(pre[at : at + hidden])
                    val = pre[at + hidden : at + 2 * hidden]
                    masked = mask * sig
                    factors[t, at : at + hidden, :] = masked * val * (1.0 - sig)
                    factors[t, at + hidden : at + 2 * hidden, :] = masked
                zn_own[t] = zn
                zhat_own[t] = zhat
                rstd_own[t] = rstd


def product_kernel(
    me_ref,
    pair2,
    pair3,
    weT,
    near_ls,
    near_rs,
    vec,
    pm,
    near_x,
    prod,
    left_sq,
    right_sq,
    zn_cols,
    far_x,
    far_ls,
    far_rs,
):
    me = me_ref[0]
    rows, tokens, _ = pair2.shape
    half = rows // 2
    hidden = weT.shape[0] // 4
    for s, ref in ((2, pair2), (3, pair3)):
        block = jnp.bitwise_xor(me, s)
        place = jnp.bitwise_and(block, 1)

        @pl.loop(0, half, unroll=8)
        def _(t, ref=ref, block=block, place=place):
            edge_tile(ref, t, block, place, weT, vec, pm, far_ls, far_rs)

        far_x[place] = ref[...].astype(F32).reshape(far_x.shape[1:])

    core = jnp.bitwise_and(me, 1)
    group = me // 2
    n_near = pl.multiple_of(group * 2 * rows, 2 * rows)
    n_far = pl.multiple_of((1 - group) * 2 * rows, 2 * rows)

    @pl.loop(0, hidden, unroll=128)
    def _(h):
        at = pl.ds(pl.multiple_of(h * half, half), half)
        for near, far, sq in ((near_ls, far_ls, left_sq), (near_rs, far_rs, right_sq)):
            sq[h, pl.ds(n_near, 2 * rows), :] = square((near[0, at, :], near[1, at, :]))
            sq[h, pl.ds(n_far, 2 * rows), :] = square((far[0, at, :], far[1, at, :]))
        prod[0, at, :] = lanes(dot_nt(halves(near_ls[core, at, :]), right_sq[h]))
        prod[1, at, :] = lanes(dot_nt(halves(near_rs[core, at, :]), left_sq[h]))

    @pl.loop(0, half, unroll=8)
    def _(t):
        x = []
        for j in (me * rows + t, me * rows + t + half):
            near, far = (
                jnp.concatenate(
                    [v[p, pl.ds(j, rows, stride=tokens), :] for p in range(2)], axis=0
                )
                for v in (near_x, far_x)
            )
            x += [jnp.where(group == 0, near, far), jnp.where(group == 0, far, near)]
        x = jnp.concatenate(x, axis=0).T
        zhat, _ = norm_columns(x)
        zn_cols[t] = (zhat * vec[0] + vec[1]).astype(BF16)


def back_kernel(
    me_ref,
    prod,
    left_sq,
    right_sq,
    zn_cols,
    factors,
    zn_own,
    zhat_own,
    pg_ref,
    pg0,
    pg1,
    pg2,
    pg3,
    we_ref,
    wg_ref,
    wo_ref,
    ogain_ref,
    obias_ref,
    dzn_ref,
    grads_ref,
    wgT,
    woT,
    vec,
    pgs,
    pr,
    dgl_own,
    xn_own,
    dy_own,
    dpre_own,
    gacc,
):
    me = me_ref[0]
    rows, tokens, width = pg_ref.shape
    half = rows // 2
    hidden = wo_ref.shape[0]
    wgT[...] = transposed(wg_ref)
    woT[...] = transposed(wo_ref)
    vec[0] = columns_of(ogain_ref)
    vec[1] = columns_of(obias_ref)
    gacc[...] = jnp.zeros_like(gacc)
    for s, ref in enumerate((pg0, pg1, pg2, pg3)):
        at = pl.multiple_of(jnp.bitwise_xor(me, s) * rows * rows, rows * rows)
        pgs[pl.ds(at, rows * rows), :] = ref[...].reshape(rows * rows, width).astype(F32)

    @pl.loop(0, half, unroll=8)
    def _(t):
        for which in range(2):
            x = prod[which, pl.ds(t, hidden, stride=half), :].astype(BF16).astype(F32)
            xhat, rstd = norm_columns(x)
            if which == 0:
                zn = zn_own[t]
                pg = two_rows(pg_ref, t)
            else:
                zn = zn_cols[t]
                pg = jnp.concatenate(
                    [
                        pgs[pl.ds(t, tokens, stride=rows), :],
                        pgs[pl.ds(t + half, tokens, stride=rows), :],
                    ],
                    axis=0,
                ).T
            gate = jax.nn.sigmoid(dot(wgT[...], zn))
            dy = (pg * gate).astype(BF16)
            dxn = dot(wo_ref[...], dy)
            if which == 0:
                xn = (xhat * vec[0] + vec[1]).astype(BF16)
                y = dot(woT[...], xn)
                dgl = (pg * y * gate * (1.0 - gate)).astype(BF16)
                dgl_own[t] = dgl
                xn_own[t] = xn
                dy_own[t] = dy
                gacc[0] += dxn * xhat
                gacc[1] += dxn
            pr[which, pl.ds(t, hidden, stride=half), :] = norm_columns_backward(
                dxn, vec[0], xhat, rstd
            )

    @pl.loop(0, hidden, unroll=128)
    def _(h):
        at = pl.ds(pl.multiple_of(h * half, half), half)
        pr[0, at, :] = lanes(dot(halves(pr[0, at, :]), right_sq[h]))
        pr[1, at, :] = lanes(dot(halves(pr[1, at, :]), left_sq[h]))

    @pl.loop(0, half, unroll=8)
    def _(t):
        zn = zn_own[t]
        zhat = zhat_own[t]
        dzn = dot(wg_ref[...], dgl_own[t])
        for which in range(2):
            d = pr[which, pl.ds(t, hidden, stride=half), :].astype(BF16).astype(F32)
            for b in (2 * which, 2 * which + 1):
                cols = slice(b * hidden, (b + 1) * hidden)
                dpre = (d * factors[t, cols, :]).astype(BF16)
                dpre_own[t, cols, :] = dpre
                dzn += dot(we_ref[:, cols], dpre)
        gacc[2] += dzn * zhat
        gacc[3] += dzn
        dzn_ref[t] = dzn

    wide = lambda ref, rows_: jnp.concatenate([ref[t, rows_, :] for t in range(half)], axis=1)
    every = slice(0, LANES)
    zn = wide(zn_own, every)
    for b in range(4):
        cols = slice(b * LANES, (b + 1) * LANES)
        grads_ref[cols, :] = dot_nt(zn, wide(dpre_own, cols)).astype(BF16)
    grads_ref[4 * LANES : 5 * LANES, :] = dot_nt(zn, wide(dgl_own, every)).astype(BF16)
    grads_ref[5 * LANES : 6 * LANES, :] = dot_nt(
        wide(xn_own, every), wide(dy_own, every)
    ).astype(BF16)
    sums = [jnp.sum(gacc[b].T, axis=0, keepdims=True) for b in (2, 3, 0, 1)]
    pad = grads_ref.shape[0] - 6 * LANES
    sums.append(jnp.zeros((pad - 4, LANES), F32))
    grads_ref[6 * LANES :, :] = jnp.concatenate(sums, axis=0).astype(BF16)


def input_kernel(me_ref, dzn_ref, zhat_own, rstd_own, vec, dz_ref):
    half = dzn_ref.shape[0]
    tokens = dz_ref.shape[1]
    gain = vec[0]
    for t in range(half):
        dz = norm_columns_backward(dzn_ref[t], gain, zhat_own[t], rstd_own[t]).T.astype(BF16)
        dz_ref[t] = dz[:tokens]
        dz_ref[t + half] = dz[tokens:]


def finish_kernel(n_blocks, me_ref, *refs):
    chunks = refs[:n_blocks]
    edges_ref, gate_ref, out_ref, in_norm_ref, out_norm_ref, total = refs[n_blocks:]
    me = me_ref[0]
    rows = chunks[0].shape[0]
    for s in range(n_blocks):
        at = pl.multiple_of(jnp.bitwise_xor(me, s) * rows, rows)
        total[pl.ds(at, rows), :] = chunks[s][...].astype(F32)
    for b in range(4):
        edges_ref[:, b * LANES : (b + 1) * LANES] = total[b * LANES : (b + 1) * LANES, :]
    gate_ref[...] = total[4 * LANES : 5 * LANES, :]
    out_ref[...] = total[5 * LANES : 6 * LANES, :]
    in_norm_ref[...] = total[6 * LANES : 6 * LANES + 2, :]
    out_norm_ref[...] = total[6 * LANES + 2 : 6 * LANES + 4, :]


def pick(x, i):
    return lax.dynamic_index_in_dim(x, i, 0, keepdims=False)


def swap(x, axis, n, bit):
    return lax.ppermute(x, axis, [(i, i ^ bit) for i in range(n)])


def bits_of(n):
    out = []
    b = n // 2
    while b:
        out.append(b)
        b //= 2
    return out


def per_device_fused(
    n_dp,
    n_dap,
    pair,
    pair_grad,
    token_mask,
    w_edges,
    w_gate,
    w_out,
    in_gain,
    in_bias,
    output_norm_gain,
    output_norm_bias,
):
    rows, tokens, width = pair.shape[1:]
    hidden = w_out.shape[0]
    me = lax.axis_index("dap")
    place = me.astype(jnp.int32).reshape(1)
    x = pair[0]
    g = pair_grad[0]

    half = rows // 2
    grad_rows = 6 * LANES + 16 * n_dap
    vm = pltpu.VMEM
    out = jax.ShapeDtypeStruct
    row = lambda v: v.reshape(1, -1)

    def call(kernel, us, outs, scratch, *args, in_hbm=0):
        whole = pl.BlockSpec(memory_space=pltpu.VMEM)
        hbm = pl.BlockSpec(memory_space=pltpu.HBM)
        return pl.pallas_call(
            kernel,
            out_shape=tuple(outs),
            in_specs=[pl.BlockSpec(memory_space=pltpu.SMEM)]
            + [whole] * (len(args) - in_hbm)
            + [hbm] * in_hbm,
            out_specs=(whole,) * len(outs),
            scratch_shapes=scratch,
            compiler_params=pltpu.CompilerParams(vmem_limit_bytes=VMEM_BYTES),
            cost_estimate=pl.CostEstimate(
                flops=0, bytes_accessed=int(us * 3.6e6), transcendentals=0
            ),
        )(place, *args)

    cut = g.reshape(rows, n_dap, rows, width)
    far = swap(x, "dap", n_dap, 2)
    near = swap(x, "dap", n_dap, 1)
    pg_own, *pgs = [lax.dynamic_index_in_dim(cut, me ^ s, 1, keepdims=False) for s in range(4)]
    pgs = [swap(v, "dap", n_dap, s) for s, v in enumerate(pgs, 1)]
    weT, ls, rs, factors, zn_own, zhat_own, rstd_own, vec, pm, near_x = call(
        near_kernel,
        4,
        [
            out((4 * hidden, width), BF16),
            out((2, hidden * half, LANES), F32),
            out((2, hidden * half, LANES), F32),
            out((half, 4 * hidden, LANES), F32),
            out((half, width, LANES), BF16),
            out((half, width, LANES), F32),
            out((half, 1, LANES), F32),
            out((2, width, LANES), F32),
            out((n_dap * half, LANES), F32),
            out((2, rows * tokens, width), F32),
        ],
        [
            vm((1, tokens), jnp.int32),
            vm((rows, tokens, width), BF16),
            vm((width, 4 * hidden), BF16),
            vm((1, width), F32),
            vm((1, width), F32),
            pltpu.SemaphoreType.DMA((5,)),
        ],
        near,
        token_mask,
        x,
        w_edges,
        row(in_gain),
        row(in_bias),
        in_hbm=5,
    )
    far, zn_own, pg_own = lax.optimization_barrier((far, zn_own, pg_own))
    across = swap(far, "dap", n_dap, 1)
    prod, left_sq, right_sq, zn_cols = call(
        product_kernel,
        8,
        [
            out((2, hidden * half, LANES), F32),
            out((hidden, tokens, tokens), BF16),
            out((hidden, tokens, tokens), BF16),
            out((half, width, LANES), BF16),
        ],
        [
            vm((2, rows * tokens, width), F32),
            vm((2, hidden * half, LANES), F32),
            vm((2, hidden * half, LANES), F32),
        ],
        far,
        across,
        weT,
        ls,
        rs,
        vec,
        pm,
        near_x,
    )
    dzn, grads = call(
        back_kernel,
        8,
        [out((half, width, LANES), F32), out((grad_rows, LANES), BF16)],
        [
            vm((width, width), BF16),
            vm((width, hidden), BF16),
            vm((2, width, LANES), F32),
            vm((n_dap * rows * rows, width), F32),
            vm((2, hidden * half, LANES), F32),
            vm((half, width, LANES), BF16),
            vm((half, hidden, LANES), BF16),
            vm((half, width, LANES), BF16),
            vm((half, 4 * hidden, LANES), BF16),
            vm((4, LANES, LANES), F32),
        ],
        prod,
        left_sq,
        right_sq,
        zn_cols,
        factors,
        zn_own,
        zhat_own,
        g,
        pg_own,
        *pgs,
        w_edges,
        w_gate,
        w_out,
        row(output_norm_gain),
        row(output_norm_bias),
    )
    (dz,) = call(
        input_kernel,
        1,
        [out((rows, tokens, width), BF16)],
        [],
        dzn,
        zhat_own,
        rstd_own,
        vec,
    )

    chunks = grads.reshape(n_dap, -1, LANES)
    total = pick(chunks, me).astype(F32)
    got = [swap(pick(chunks, me ^ s), "dap", n_dap, s) for s in range(1, n_dap)]
    for c in got:
        total = total + c.astype(F32)
    total = total.astype(BF16)
    bits = bits_of(n_dp)[::-1]
    for i in range(0, len(bits), 2):
        terms = [total.astype(F32)]
        shifts = [0]
        for bit in bits[i : i + 2]:
            shifts += [s ^ bit for s in shifts]
        terms += [swap(total, "dp", n_dp, s).astype(F32) for s in shifts[1:]]
        while len(terms) > 1:
            terms = [p + q for p, q in zip(terms[::2], terms[1::2])]
        total = terms[0].astype(BF16)
    parts = [total] + [swap(total, "dap", n_dap, s) for s in range(1, n_dap)]
    edges, gate, outs, in_norm, out_norm = call(
        functools.partial(finish_kernel, n_dap),
        1,
        [
            out((width, 4 * hidden), F32),
            out((width, width), F32),
            out((hidden, width), F32),
            out((2, width), F32),
            out((2, hidden), F32),
        ],
        [vm((grad_rows, LANES), F32)],
        *parts,
    )
    return (dz[None], edges, gate, outs, in_norm, out_norm)


def solution(mesh):
    in_specs = (
        P("dp", "dap", None, None),
        P("dp", "dap", None, None),
        P("dp", None),
        P(),
        P(),
        P(),
        P(),
        P(),
        P(),
        P(),
    )
    out_specs = (P("dp", "dap", None, None), P(), P(), P(), P(), P())
    n_dp, n_dap = mesh.shape["dp"], mesh.shape["dap"]

    def per_device(pair, *others):
        structs, rows, tokens, width = pair.shape
        hidden = others[4].shape[0]
        fits = (
            structs == 1
            and 2 * tokens == LANES
            and rows == 16
            and width == LANES
            and hidden == LANES
            and n_dap == 4
            and n_dp & (n_dp - 1) == 0
        )
        if fits:
            return per_device_fused(n_dp, n_dap, pair, *others)
        return per_device_exchange(pair, *others)

    return jax.shard_map(
        per_device, mesh=mesh, in_specs=in_specs, out_specs=out_specs, check_vma=False
    )
```

```python
import functools

import jax
import jax.numpy as jnp
from jax import lax
from jax.experimental import pallas as pl
from jax.experimental.pallas import tpu as pltpu
from jax.sharding import PartitionSpec as P

EPS = 1e-05
LANES = 128
VMEM_BYTES = 32 * 1024 * 1024
F32 = jnp.float32
BF16 = jnp.bfloat16


def apply_layer_norm(values, reduce_dimension):
    mean = jnp.mean(values, axis=reduce_dimension, keepdims=True)
    var = jnp.mean((values - mean) ** 2, axis=reduce_dimension, keepdims=True)
    rstd = lax.rsqrt(var + EPS)
    return ((values - mean) * rstd, rstd)


def layer_norm_backward(dnorm, gain, normed, rstd, reduce_dimension):
    scaled = dnorm * gain
    return (
        scaled
        - jnp.mean(scaled, axis=reduce_dimension, keepdims=True)
        - normed * jnp.mean(scaled * normed, axis=reduce_dimension, keepdims=True)
    ) * rstd


def per_device_exchange(
    pair,
    pair_grad,
    token_mask,
    w_edges,
    w_gate,
    w_out,
    in_gain,
    in_bias,
    output_norm_gain,
    output_norm_bias,
):
    z_rows = pair[0]
    dout = pair_grad[0]
    rows = z_rows.shape[0]
    hidden = w_out.shape[0]
    width = w_gate.shape[0]
    first = lax.axis_index("dap") * rows
    mask_full = token_mask[0].astype(jnp.float32)
    mask_rows = lax.dynamic_slice_in_dim(mask_full, first, rows, 0)
    edge_mask = mask_rows[:, None, None] * mask_full[None, None, :]
    zhat, rstd_in = apply_layer_norm(z_rows.astype(jnp.float32), 2)
    zn = (zhat * in_gain + in_bias).astype(jnp.bfloat16)

    def project(columns):
        return jnp.einsum("ikc,ch->ihk", zn, columns, preferred_element_type=jnp.float32)

    def edge_values(pre):
        return (edge_mask * jax.nn.sigmoid(pre[:, :hidden]) * pre[:, hidden:]).astype(jnp.bfloat16)

    pre_left = project(w_edges[:, : 2 * hidden])
    pre_right = project(w_edges[:, 2 * hidden :])
    left_ch, right_ch = (
        lax.all_to_all(edge_values(pre_left), "dap", split_axis=1, concat_axis=0, tiled=True),
        lax.all_to_all(edge_values(pre_right), "dap", split_axis=1, concat_axis=0, tiled=True),
    )
    tri = jnp.einsum("ihk,jhk->ihj", left_ch, right_ch, preferred_element_type=jnp.float32).astype(
        jnp.bfloat16
    )
    triangle_product = lax.all_to_all(tri, "dap", split_axis=0, concat_axis=1, tiled=True)
    centered_scaled_input, output_inverse_deviation = apply_layer_norm(
        triangle_product.astype(jnp.float32), 1
    )
    normalized_product = (
        centered_scaled_input * output_norm_gain[None, :, None] + output_norm_bias[None, :, None]
    ).astype(jnp.bfloat16)
    gate = jax.nn.sigmoid(jnp.einsum("ijc,cd->ijd", zn, w_gate, preferred_element_type=jnp.float32))
    y_out = jnp.einsum("ihj,hc->ijc", normalized_product, w_out, preferred_element_type=jnp.float32)
    doutf = dout.astype(jnp.float32)
    dy = (doutf * gate).astype(jnp.bfloat16)
    dgl = (doutf * y_out * gate * (1.0 - gate)).astype(jnp.bfloat16)
    grad_out = jnp.einsum("ihj,ijc->hc", normalized_product, dy, preferred_element_type=jnp.float32)
    normalized_gradient = jnp.einsum("ijc,hc->ihj", dy, w_out, preferred_element_type=jnp.float32)
    output_norm_backward = jnp.stack(
        [
            jnp.sum(normalized_gradient * centered_scaled_input, axis=(0, 2)),
            jnp.sum(normalized_gradient, axis=(0, 2)),
        ]
    )
    product_gradient = layer_norm_backward(
        normalized_gradient,
        output_norm_gain[None, :, None],
        centered_scaled_input,
        output_inverse_deviation,
        1,
    ).astype(jnp.bfloat16)
    dprod_ch = lax.all_to_all(product_gradient, "dap", split_axis=1, concat_axis=0, tiled=True)
    dleft_ch = jnp.einsum(
        "ihj,jhk->ihk", dprod_ch, right_ch, preferred_element_type=jnp.float32
    ).astype(jnp.bfloat16)
    dright_ch = jnp.einsum(
        "ihj,ihk->jhk", dprod_ch, left_ch, preferred_element_type=jnp.float32
    ).astype(jnp.bfloat16)
    dleft, dright = (
        lax.all_to_all(dleft_ch, "dap", split_axis=0, concat_axis=1, tiled=True),
        lax.all_to_all(dright_ch, "dap", split_axis=0, concat_axis=1, tiled=True),
    )

    def pre_grad(dvalues, pre):
        sig = jax.nn.sigmoid(pre[:, :hidden])
        masked = dvalues.astype(jnp.float32) * edge_mask
        return jnp.concatenate(
            [masked * pre[:, hidden:] * sig * (1.0 - sig), masked * sig], axis=1
        ).astype(jnp.bfloat16)

    dpre_left = pre_grad(dleft, pre_left)
    dpre_right = pre_grad(dright, pre_right)
    grad_edges = jnp.concatenate(
        [
            jnp.einsum("ikc,ihk->ch", zn, dpre_left, preferred_element_type=jnp.float32),
            jnp.einsum("ikc,ihk->ch", zn, dpre_right, preferred_element_type=jnp.float32),
        ],
        axis=1,
    )
    grad_gate = jnp.einsum("ijc,ijd->cd", zn, dgl, preferred_element_type=jnp.float32)
    dzn = jnp.einsum(
        "ihk,ch->ikc", dpre_left, w_edges[:, : 2 * hidden], preferred_element_type=jnp.float32
    )
    dzn = dzn + jnp.einsum(
        "ihk,ch->ikc", dpre_right, w_edges[:, 2 * hidden :], preferred_element_type=jnp.float32
    )
    dzn = dzn + jnp.einsum("ijd,cd->ijc", dgl, w_gate, preferred_element_type=jnp.float32)
    in_norm_grad = jnp.stack([jnp.sum(dzn * zhat, axis=(0, 1)), jnp.sum(dzn, axis=(0, 1))])
    dz = layer_norm_backward(dzn, in_gain, zhat, rstd_in, 2).astype(jnp.bfloat16)
    flat = jnp.concatenate(
        [
            grad_edges.ravel(),
            grad_gate.ravel(),
            grad_out.ravel(),
            in_norm_grad.ravel(),
            output_norm_backward.ravel(),
        ]
    )
    summed = lax.psum(flat, ("dp", "dap"))
    edge_size = width * 4 * hidden
    gate_size = width * width
    out_size = hidden * width
    offset = 0
    total_edges = summed[offset : offset + edge_size].reshape(width, 4 * hidden)
    offset = offset + edge_size
    total_gate = summed[offset : offset + gate_size].reshape(width, width)
    offset = offset + gate_size
    total_out = summed[offset : offset + out_size].reshape(hidden, width)
    offset = offset + out_size
    total_in_norm = summed[offset : offset + 2 * width].reshape(2, width)
    offset = offset + 2 * width
    total_out_norm = summed[offset : offset + 2 * hidden].reshape(2, hidden)
    return (dz[None], total_edges, total_gate, total_out, total_in_norm, total_out_norm)


def dot(a, b):
    return jnp.dot(a, b, preferred_element_type=F32)


def dot_nt(a, b):
    return lax.dot_general(a, b, (((1,), (1,)), ((), ())), preferred_element_type=F32)


def norm_columns(x):
    mean = jnp.mean(x, axis=0, keepdims=True)
    centred = x - mean
    var = jnp.mean(centred * centred, axis=0, keepdims=True)
    rstd = lax.rsqrt(var + EPS)
    return centred * rstd, rstd


def norm_columns_backward(dnorm, gain, normed, rstd):
    scaled = dnorm * gain
    m1 = jnp.mean(scaled, axis=0, keepdims=True)
    m2 = jnp.mean(scaled * normed, axis=0, keepdims=True)
    return (scaled - m1 - normed * m2) * rstd


def halves(x):
    n = LANES // 2
    return jnp.concatenate([x[:, :n], x[:, n:]], axis=0).astype(BF16)


def lanes(x):
    return jnp.concatenate([x[:8], x[8:]], axis=1)


def square(blocks):
    n = LANES // 2
    return jnp.concatenate([p for x in blocks for p in (x[:, :n], x[:, n:])], axis=0).astype(BF16)


def columns_of(ref):
    return jnp.broadcast_to(ref[...], (ref.shape[1], LANES)).T


def transposed(ref):
    return ref[...].astype(F32).T.astype(BF16)


def fill_pair_mask(mask_ref, pm, rows):
    half = rows // 2
    low = lax.broadcasted_iota(jnp.int32, (half, LANES), 1) < LANES // 2
    m = mask_ref[...].astype(F32)
    m = jnp.broadcast_to(jnp.concatenate([m, m], axis=1), (LANES, LANES))
    mt = m.T
    for a in range(pm.shape[0] // half):
        lo = mt[rows * a : rows * a + half]
        hi = mt[rows * a + half : rows * (a + 1)]
        pm[half * a : half * (a + 1), :] = jnp.where(low, lo, hi) * m[:half]


def two_rows(ref, t):
    half = ref.shape[0] // 2
    return jnp.concatenate([ref[t].astype(F32), ref[t + half].astype(F32)], axis=0).T


def edge_tile(pair_ref, t, block, place, weT, vec, pm, ls, rs):
    half = pair_ref.shape[0] // 2
    hidden = weT.shape[0] // 4
    zhat, rstd = norm_columns(two_rows(pair_ref, t))
    zn = (zhat * vec[0] + vec[1]).astype(BF16)
    pre = dot(weT[...], zn)
    mask = pm[pl.ds(block * half + t, 1), :]
    ls[place, pl.ds(t, hidden, stride=half), :] = (
        mask * jax.nn.sigmoid(pre[:hidden]) * pre[hidden : 2 * hidden]
    )
    rs[place, pl.ds(t, hidden, stride=half), :] = (
        mask * jax.nn.sigmoid(pre[2 * hidden : 3 * hidden]) * pre[3 * hidden :]
    )
    return zhat, rstd, zn, pre


def near_kernel(
    me_ref,
    near_ref,
    mask_hbm,
    own_hbm,
    we_hbm,
    gain_hbm,
    bias_hbm,
    weT,
    ls,
    rs,
    factors,
    zn_own,
    zhat_own,
    rstd_own,
    vec,
    pm,
    near_x,
    mask_ref,
    own_ref,
    we_ref,
    gain_ref,
    bias_ref,
    sems,
):
    me = me_ref[0]
    copies = [
        pltpu.make_async_copy(src, dst, sems.at[i])
        for i, (src, dst) in enumerate(
            (
                (we_hbm, we_ref),
                (own_hbm, own_ref),
                (mask_hbm, mask_ref),
                (gain_hbm, gain_ref),
                (bias_hbm, bias_ref),
            )
        )
    ]
    for copy in copies:
        copy.start()
    for copy in copies:
        copy.wait()
    rows = own_ref.shape[0]
    half = rows // 2
    hidden = we_ref.shape[1] // 4
    for b in range(4):
        cols = slice(b * hidden, (b + 1) * hidden)
        weT[cols, :] = we_ref[:, cols].astype(F32).T.astype(BF16)
    vec[0] = columns_of(gain_ref)
    vec[1] = columns_of(bias_ref)
    fill_pair_mask(mask_ref, pm, rows)
    for s, ref in enumerate((own_ref, near_ref)):
        block = jnp.bitwise_xor(me, s)
        place = jnp.bitwise_and(block, 1)
        near_x[place] = ref[...].astype(F32).reshape(near_x.shape[1:])

        @pl.loop(0, half, unroll=8)
        def _(t, s=s, ref=ref, block=block, place=place):
            zhat, rstd, zn, pre = edge_tile(ref, t, block, place, weT, vec, pm, ls, rs)
            if s == 0:
                mask = pm[pl.ds(block * half + t, 1), :]
                for which in range(2):
                    at = 2 * which * hidden
                    sig = jax.nn.sigmoid(pre[at : at + hidden])
                    val = pre[at + hidden : at + 2 * hidden]
                    masked = mask * sig
                    factors[t, at : at + hidden, :] = masked * val * (1.0 - sig)
                    factors[t, at + hidden : at + 2 * hidden, :] = masked
                zn_own[t] = zn
                zhat_own[t] = zhat
                rstd_own[t] = rstd


def product_kernel(
    me_ref,
    pair2,
    pair3,
    weT,
    near_ls,
    near_rs,
    vec,
    pm,
    near_x,
    prod,
    left_sq,
    right_sq,
    zn_cols,
    far_x,
    far_ls,
    far_rs,
):
    me = me_ref[0]
    rows, tokens, _ = pair2.shape
    half = rows // 2
    hidden = weT.shape[0] // 4
    for s, ref in ((2, pair2), (3, pair3)):
        block = jnp.bitwise_xor(me, s)
        place = jnp.bitwise_and(block, 1)

        @pl.loop(0, half, unroll=8)
        def _(t, ref=ref, block=block, place=place):
            edge_tile(ref, t, block, place, weT, vec, pm, far_ls, far_rs)

        far_x[place] = ref[...].astype(F32).reshape(far_x.shape[1:])

    core = jnp.bitwise_and(me, 1)
    group = me // 2
    n_near = pl.multiple_of(group * 2 * rows, 2 * rows)
    n_far = pl.multiple_of((1 - group) * 2 * rows, 2 * rows)

    @pl.loop(0, hidden, unroll=128)
    def _(h):
        at = pl.ds(pl.multiple_of(h * half, half), half)
        for near, far, sq in ((near_ls, far_ls, left_sq), (near_rs, far_rs, right_sq)):
            sq[h, pl.ds(n_near, 2 * rows), :] = square((near[0, at, :], near[1, at, :]))
            sq[h, pl.ds(n_far, 2 * rows), :] = square((far[0, at, :], far[1, at, :]))
        prod[0, at, :] = lanes(dot_nt(halves(near_ls[core, at, :]), right_sq[h]))
        prod[1, at, :] = lanes(dot_nt(halves(near_rs[core, at, :]), left_sq[h]))

    @pl.loop(0, half, unroll=8)
    def _(t):
        x = []
        for j in (me * rows + t, me * rows + t + half):
            near, far = (
                jnp.concatenate(
                    [v[p, pl.ds(j, rows, stride=tokens), :] for p in range(2)], axis=0
                )
                for v in (near_x, far_x)
            )
            x += [jnp.where(group == 0, near, far), jnp.where(group == 0, far, near)]
        x = jnp.concatenate(x, axis=0).T
        zhat, _ = norm_columns(x)
        zn_cols[t] = (zhat * vec[0] + vec[1]).astype(BF16)


def back_kernel(
    me_ref,
    prod,
    left_sq,
    right_sq,
    zn_cols,
    factors,
    zn_own,
    zhat_own,
    pg_ref,
    pg0,
    pg1,
    pg2,
    pg3,
    we_ref,
    wg_ref,
    wo_ref,
    ogain_ref,
    obias_ref,
    dzn_ref,
    grads_ref,
    wgT,
    woT,
    vec,
    pgs,
    pr,
    dgl_own,
    xn_own,
    dy_own,
    dpre_own,
    gacc,
):
    me = me_ref[0]
    rows, tokens, width = pg_ref.shape
    half = rows // 2
    hidden = wo_ref.shape[0]
    wgT[...] = transposed(wg_ref)
    woT[...] = transposed(wo_ref)
    vec[0] = columns_of(ogain_ref)
    vec[1] = columns_of(obias_ref)
    gacc[...] = jnp.zeros_like(gacc)
    for s, ref in enumerate((pg0, pg1, pg2, pg3)):
        at = pl.multiple_of(jnp.bitwise_xor(me, s) * rows * rows, rows * rows)
        pgs[pl.ds(at, rows * rows), :] = ref[...].reshape(rows * rows, width).astype(F32)

    @pl.loop(0, half, unroll=8)
    def _(t):
        for which in range(2):
            x = prod[which, pl.ds(t, hidden, stride=half), :].astype(BF16).astype(F32)
            xhat, rstd = norm_columns(x)
            if which == 0:
                zn = zn_own[t]
                pg = two_rows(pg_ref, t)
            else:
                zn = zn_cols[t]
                pg = jnp.concatenate(
                    [
                        pgs[pl.ds(t, tokens, stride=rows), :],
                        pgs[pl.ds(t + half, tokens, stride=rows), :],
                    ],
                    axis=0,
                ).T
            gate = jax.nn.sigmoid(dot(wgT[...], zn))
            dy = (pg * gate).astype(BF16)
            dxn = dot(wo_ref[...], dy)
            if which == 0:
                xn = (xhat * vec[0] + vec[1]).astype(BF16)
                y = dot(woT[...], xn)
                dgl = (pg * y * gate * (1.0 - gate)).astype(BF16)
                dgl_own[t] = dgl
                xn_own[t] = xn
                dy_own[t] = dy
                gacc[0] += dxn * xhat
                gacc[1] += dxn
            pr[which, pl.ds(t, hidden, stride=half), :] = norm_columns_backward(
                dxn, vec[0], xhat, rstd
            )

    @pl.loop(0, hidden, unroll=128)
    def _(h):
        at = pl.ds(pl.multiple_of(h * half, half), half)
        pr[0, at, :] = lanes(dot(halves(pr[0, at, :]), right_sq[h]))
        pr[1, at, :] = lanes(dot(halves(pr[1, at, :]), left_sq[h]))

    @pl.loop(0, half, unroll=8)
    def _(t):
        zn = zn_own[t]
        zhat = zhat_own[t]
        dzn = dot(wg_ref[...], dgl_own[t])
        for which in range(2):
            d = pr[which, pl.ds(t, hidden, stride=half), :].astype(BF16).astype(F32)
            for b in (2 * which, 2 * which + 1):
                cols = slice(b * hidden, (b + 1) * hidden)
                dpre = (d * factors[t, cols, :]).astype(BF16)
                dpre_own[t, cols, :] = dpre
                dzn += dot(we_ref[:, cols], dpre)
        gacc[2] += dzn * zhat
        gacc[3] += dzn
        dzn_ref[t] = dzn

    wide = lambda ref, rows_: jnp.concatenate([ref[t, rows_, :] for t in range(half)], axis=1)
    every = slice(0, LANES)
    zn = wide(zn_own, every)
    for b in range(4):
        cols = slice(b * LANES, (b + 1) * LANES)
        grads_ref[cols, :] = dot_nt(zn, wide(dpre_own, cols)).astype(BF16)
    grads_ref[4 * LANES : 5 * LANES, :] = dot_nt(zn, wide(dgl_own, every)).astype(BF16)
    grads_ref[5 * LANES : 6 * LANES, :] = dot_nt(
        wide(xn_own, every), wide(dy_own, every)
    ).astype(BF16)
    sums = [jnp.sum(gacc[b].T, axis=0, keepdims=True) for b in (2, 3, 0, 1)]
    pad = grads_ref.shape[0] - 6 * LANES
    sums.append(jnp.zeros((pad - 4, LANES), F32))
    grads_ref[6 * LANES :, :] = jnp.concatenate(sums, axis=0).astype(BF16)


def input_kernel(me_ref, dzn_ref, zhat_own, rstd_own, vec, dz_ref):
    half = dzn_ref.shape[0]
    tokens = dz_ref.shape[1]
    gain = vec[0]
    for t in range(half):
        dz = norm_columns_backward(dzn_ref[t], gain, zhat_own[t], rstd_own[t]).T.astype(BF16)
        dz_ref[t] = dz[:tokens]
        dz_ref[t + half] = dz[tokens:]


def finish_kernel(n_blocks, me_ref, *refs):
    chunks = refs[:n_blocks]
    edges_ref, gate_ref, out_ref, in_norm_ref, out_norm_ref, total = refs[n_blocks:]
    me = me_ref[0]
    rows = chunks[0].shape[0]
    for s in range(n_blocks):
        at = pl.multiple_of(jnp.bitwise_xor(me, s) * rows, rows)
        total[pl.ds(at, rows), :] = chunks[s][...].astype(F32)
    for b in range(4):
        edges_ref[:, b * LANES : (b + 1) * LANES] = total[b * LANES : (b + 1) * LANES, :]
    gate_ref[...] = total[4 * LANES : 5 * LANES, :]
    out_ref[...] = total[5 * LANES : 6 * LANES, :]
    in_norm_ref[...] = total[6 * LANES : 6 * LANES + 2, :]
    out_norm_ref[...] = total[6 * LANES + 2 : 6 * LANES + 4, :]


def pick(x, i):
    return lax.dynamic_index_in_dim(x, i, 0, keepdims=False)


def swap(x, axis, n, bit):
    return lax.ppermute(x, axis, [(i, i ^ bit) for i in range(n)])


def bits_of(n):
    out = []
    b = n // 2
    while b:
        out.append(b)
        b //= 2
    return out


def per_device_fused(
    n_dp,
    n_dap,
    pair,
    pair_grad,
    token_mask,
    w_edges,
    w_gate,
    w_out,
    in_gain,
    in_bias,
    output_norm_gain,
    output_norm_bias,
):
    rows, tokens, width = pair.shape[1:]
    hidden = w_out.shape[0]
    me = lax.axis_index("dap")
    place = me.astype(jnp.int32).reshape(1)
    x = pair[0]
    g = pair_grad[0]

    half = rows // 2
    grad_rows = 6 * LANES + 16 * n_dap
    vm = pltpu.VMEM
    out = jax.ShapeDtypeStruct
    row = lambda v: v.reshape(1, -1)

    def call(kernel, us, outs, scratch, *args, in_hbm=0):
        whole = pl.BlockSpec(memory_space=pltpu.VMEM)
        hbm = pl.BlockSpec(memory_space=pltpu.HBM)
        return pl.pallas_call(
            kernel,
            out_shape=tuple(outs),
            in_specs=[pl.BlockSpec(memory_space=pltpu.SMEM)]
            + [whole] * (len(args) - in_hbm)
            + [hbm] * in_hbm,
            out_specs=(whole,) * len(outs),
            scratch_shapes=scratch,
            compiler_params=pltpu.CompilerParams(vmem_limit_bytes=VMEM_BYTES),
            cost_estimate=pl.CostEstimate(
                flops=0, bytes_accessed=int(us * 3.6e6), transcendentals=0
            ),
        )(place, *args)

    cut = g.reshape(rows, n_dap, rows, width)
    far = swap(x, "dap", n_dap, 2)
    near = swap(x, "dap", n_dap, 1)
    pg_own, *pgs = [lax.dynamic_index_in_dim(cut, me ^ s, 1, keepdims=False) for s in range(4)]
    pgs = [swap(v, "dap", n_dap, s) for s, v in enumerate(pgs, 1)]
    weT, ls, rs, factors, zn_own, zhat_own, rstd_own, vec, pm, near_x = call(
        near_kernel,
        4,
        [
            out((4 * hidden, width), BF16),
            out((2, hidden * half, LANES), F32),
            out((2, hidden * half, LANES), F32),
            out((half, 4 * hidden, LANES), F32),
            out((half, width, LANES), BF16),
            out((half, width, LANES), F32),
            out((half, 1, LANES), F32),
            out((2, width, LANES), F32),
            out((n_dap * half, LANES), F32),
            out((2, rows * tokens, width), F32),
        ],
        [
            vm((1, tokens), jnp.int32),
            vm((rows, tokens, width), BF16),
            vm((width, 4 * hidden), BF16),
            vm((1, width), F32),
            vm((1, width), F32),
            pltpu.SemaphoreType.DMA((5,)),
        ],
        near,
        token_mask,
        x,
        w_edges,
        row(in_gain),
        row(in_bias),
        in_hbm=5,
    )
    far, zn_own, pg_own, pgs[0] = lax.optimization_barrier((far, zn_own, pg_own, pgs[0]))
    across = swap(far, "dap", n_dap, 1)
    prod, left_sq, right_sq, zn_cols = call(
        product_kernel,
        8,
        [
            out((2, hidden * half, LANES), F32),
            out((hidden, tokens, tokens), BF16),
            out((hidden, tokens, tokens), BF16),
            out((half, width, LANES), BF16),
        ],
        [
            vm((2, rows * tokens, width), F32),
            vm((2, hidden * half, LANES), F32),
            vm((2, hidden * half, LANES), F32),
        ],
        far,
        across,
        weT,
        ls,
        rs,
        vec,
        pm,
        near_x,
    )
    dzn, grads = call(
        back_kernel,
        8,
        [out((half, width, LANES), F32), out((grad_rows, LANES), BF16)],
        [
            vm((width, width), BF16),
            vm((width, hidden), BF16),
            vm((2, width, LANES), F32),
            vm((n_dap * rows * rows, width), F32),
            vm((2, hidden * half, LANES), F32),
            vm((half, width, LANES), BF16),
            vm((half, hidden, LANES), BF16),
            vm((half, width, LANES), BF16),
            vm((half, 4 * hidden, LANES), BF16),
            vm((4, LANES, LANES), F32),
        ],
        prod,
        left_sq,
        right_sq,
        zn_cols,
        factors,
        zn_own,
        zhat_own,
        g,
        pg_own,
        *pgs,
        w_edges,
        w_gate,
        w_out,
        row(output_norm_gain),
        row(output_norm_bias),
    )
    (dz,) = call(
        input_kernel,
        1,
        [out((rows, tokens, width), BF16)],
        [],
        dzn,
        zhat_own,
        rstd_own,
        vec,
    )

    chunks = grads.reshape(n_dap, -1, LANES)
    total = pick(chunks, me).astype(F32)
    got = [swap(pick(chunks, me ^ s), "dap", n_dap, s) for s in range(n_dap - 1, 0, -1)]
    for c in got:
        total = total + c.astype(F32)
    total = total.astype(BF16)
    bits = bits_of(n_dp)[::-1]
    for i in range(0, len(bits), 2):
        terms = [total.astype(F32)]
        shifts = [0]
        for bit in bits[i : i + 2]:
            shifts += [s ^ bit for s in shifts]
        terms += [swap(total, "dp", n_dp, s).astype(F32) for s in shifts[1:]]
        while len(terms) > 1:
            terms = [p + q for p, q in zip(terms[::2], terms[1::2])]
        total = terms[0].astype(BF16)
    parts = {s: swap(total, "dap", n_dap, s) for s in range(n_dap - 1, 0, -1)}
    parts = [total] + [parts[s] for s in range(1, n_dap)]
    edges, gate, outs, in_norm, out_norm = call(
        functools.partial(finish_kernel, n_dap),
        1,
        [
            out((width, 4 * hidden), F32),
            out((width, width), F32),
            out((hidden, width), F32),
            out((2, width), F32),
            out((2, hidden), F32),
        ],
        [vm((grad_rows, LANES), F32)],
        *parts,
    )
    return (dz[None], edges, gate, outs, in_norm, out_norm)


def solution(mesh):
    in_specs = (
        P("dp", "dap", None, None),
        P("dp", "dap", None, None),
        P("dp", None),
        P(),
        P(),
        P(),
        P(),
        P(),
        P(),
        P(),
    )
    out_specs = (P("dp", "dap", None, None), P(), P(), P(), P(), P())
    n_dp, n_dap = mesh.shape["dp"], mesh.shape["dap"]

    def per_device(pair, *others):
        structs, rows, tokens, width = pair.shape
        hidden = others[4].shape[0]
        fits = (
            structs == 1
            and 2 * tokens == LANES
            and rows == 16
            and width == LANES
            and hidden == LANES
            and n_dap == 4
            and n_dp & (n_dp - 1) == 0
        )
        if fits:
            return per_device_fused(n_dp, n_dap, pair, *others)
        return per_device_exchange(pair, *others)

    return jax.shard_map(
        per_device, mesh=mesh, in_specs=in_specs, out_specs=out_specs, check_vma=False
    )
```
